256 devices in a mesh: ckpt: 16 (over x, z_hi), tensor: 16 (over z_lo, y, core).
Axes of the slice: x: 4, y: 4, z: 8 (z_hi: 4, z_lo: 2; z = z_hi * 2 + z_lo), core: 2. Of those that a mesh axis runs over, the one named last changes fastest.
Arguments:
- acts: bfloat16 [16, 2048, 3584], P('ckpt', 'tensor'), may hold values from -6 to 6
- cotangent: bfloat16 [16, 2048, 8192], P('ckpt', None, 'tensor'), may hold values from -0.29882812 to 0.29882812
- seq_lengths: int32 [4], replicated, may hold values from 1 to 512, 1536 in all
- up_weight: bfloat16 [16, 3584, 8192], P('ckpt', None, 'tensor'), may hold values from -0.125 to 0.125
Outputs:
- merged: bfloat16 [3584, 8192], P(None, 'tensor')
The draws below stay inside these ranges and needn't reach their ends.
All inputs are finite; a program needn't handle non-finite values.
Results may differ from the reference program's by a relative error of at most 0.001.
Values may be sent and summed in bfloat16 or wider, within the bound.
A program may use at most 128 MiB of HBM per device.

```python
import math
import jax
import jax.numpy as jnp
import numpy as np
from jax import lax

D = 3584
FFW = 8192
SEQS = 4
LEN = 512
TOKENS = 2048
MODELS = 16


def with_spikes(values, key, source, target, shards_of, factor):
    def block_of(position):
        return (jnp.arange(values.shape[position]) // (values.shape[position] // shards_of)).reshape((-1,) + (1,) * (values.ndim - 1 - position))

    near = jax.random.permutation(key, shards_of)[block_of(target)]
    other_side = (block_of(target) + shards_of // 2) % shards_of
    return jnp.where((block_of(source) == near) | (block_of(source) == other_side), factor * values, values)


def block_scale(stream_key, dims, split, low, high):
    loudness, own = 1.0, jax.random.fold_in(stream_key, 6)
    for dim, shards_of in split:
        steps = jnp.exp(jax.random.uniform(jax.random.fold_in(own, dim), (shards_of,), jnp.float32, low / len(split), high / len(split)))
        loudness = loudness * jnp.repeat(steps, dims[dim] // shards_of).reshape([-1 if axis == dim else 1 for axis in range(len(dims))])
    return loudness


def split_up(number_of, total, most, slope):
    loads = [(1 << 20) // math.isqrt(standing ** slope) + 1 for standing in range(2, number_of + 1)]
    rest, holding = total - most - (number_of - 1), [1] * (number_of - 1)
    while rest > 0:
        free = [i for i in range(number_of - 1) if holding[i] < most]
        whole, left = sum([loads[i] for i in free]), rest
        for i in free:
            more = min(most - holding[i], max(1, left * loads[i] // whole), rest)
            holding[i] = holding[i] + more
            rest = rest - more
    return np.array([most] + holding)


def uneven(own_key, amount, total, reach, lean):
    if amount == 2:
        one = jax.random.randint(own_key, (), max(1, total - reach), min(reach, total - 1) + 1)
        return jnp.stack([one, total - one])
    tallies = jnp.asarray(split_up(amount, total, reach, lean), jnp.int32)
    couples = (amount - 1) // 2
    source_of, receiver = tallies[1:1 + 2 * couples:2], tallies[2:2 + 2 * couples:2]
    room = jnp.minimum(source_of - 1, reach - receiver)
    passed = jax.random.randint(jax.random.fold_in(own_key, 1), (couples,), 0, 1 << 20) % (room + 1)
    tallies = tallies.at[1:1 + 2 * couples:2].set(source_of - passed).at[2:2 + 2 * couples:2].set(receiver + passed)
    return tallies[jax.random.permutation(jax.random.fold_in(own_key, 2), amount)]


def noise(stream_key, shape, width, limit, split=(), held_as=jnp.bfloat16):
    drawn = jax.random.normal(stream_key, shape, jnp.float32) * width
    if len(split) > 0:
        drawn = block_scale(stream_key, shape, split, -0.22, 0.18) * drawn
    return jnp.clip(drawn, min=-limit, max=limit).astype(held_as)


def bell_draw_with(stream_key, dims, width, reach, split, heavy, held_as=jnp.bfloat16):
    array = width * jax.random.normal(stream_key, dims, jnp.float32)
    if split:
        array = array * block_scale(stream_key, dims, split, -0.22, 0.18)
    return jnp.clip(with_spikes(array, jax.random.fold_in(stream_key, 3), *heavy), -reach, reach).astype(held_as)


def setup_inputs(seed: int = 0) -> dict:
    arg_keys = jax.random.split(jax.random.key(seed), 5)
    acts = noise(arg_keys[0], (MODELS, TOKENS, D), 1.0, 6.0, ((0, 16), (1, 16)))
    cotangent = noise(arg_keys[1], (MODELS, TOKENS, FFW), 0.05, 0.29882812, ((0, 16), (2, 16)))
    seq_lengths = uneven(arg_keys[2], SEQS, SEQS * LEN * 3 // 4, LEN, 0).astype(jnp.int32)
    up_weight = bell_draw_with(arg_keys[3], (MODELS, D, FFW), D ** -0.5, 0.125, ((0, 16), (2, 16)), (0, 1, 16, 2.0))
    return dict(acts=acts, cotangent=cotangent, seq_lengths=seq_lengths, up_weight=up_weight)


def model_fisher(inputs, grads, seq_lengths):
    positions = jnp.arange(LEN, dtype=jnp.int32)
    live = positions[None, :] < seq_lengths[:, None]
    shaped_in = inputs.reshape(SEQS, LEN, D)
    shaped_g = grads.reshape(SEQS, LEN, FFW)
    shaped_g = jnp.where(live[:, :, None], shaped_g, jnp.zeros_like(shaped_g))

    def one_seq(total, pair):
        x_rows, g_rows = pair
        grad = jnp.dot(x_rows.T, g_rows, preferred_element_type=jnp.float32)
        return total + grad * grad, None

    start = jnp.zeros((D, FFW), jnp.float32)
    total, unused = lax.scan(one_seq, start, (shaped_in, shaped_g))
    return total


def reference(acts, cotangent, seq_lengths, up_weight):
    def one_model(carry, trio):
        numer, denom = carry
        inputs, grads, weight = trio
        fisher = model_fisher(inputs, grads, seq_lengths)
        return (numer + fisher * weight.astype(jnp.float32), denom + fisher), None

    zeros = jnp.zeros((D, FFW), jnp.float32)
    (numer, denom), unused = lax.scan(one_model, (zeros, zeros), (acts, cotangent, up_weight))
    return (numer / (denom + 1e-6)).astype(jnp.bfloat16)
```

```python
import jax
import jax.numpy as jnp
from jax import lax
from jax.experimental import pallas as pl
from jax.experimental.pallas import tpu as pltpu
from jax.sharding import PartitionSpec as P

MESH = pl.DeviceIdType.MESH
F32, BF16, I16, I32 = jnp.float32, jnp.bfloat16, jnp.int16, jnp.int32
UNITS = 14
ROWS = 256
LANES = 128
TILE = 16
SLOTS = 4
D_TOP = 65504.0
D_MID = 32752
R_TOP = 32704.0
W_MAX = 0.125


def fourth_root(v):
    return jnp.sqrt(jnp.sqrt(v))


def wide(tile, count):
    return jnp.concatenate([tile] * count, axis=1)


def scale_of(exponent):
    return jnp.exp2(exponent.astype(F32))


def code_d(v, inverse):
    root = fourth_root(v * inverse)
    code = (root * D_TOP + 0.5).astype(I32) - D_MID
    return jnp.minimum(code, 32767).astype(I16)


def read_d(code, scale):
    root = (code.astype(F32) + float(D_MID)) * (1.0 / D_TOP)
    square = root * root
    return square * square * scale


def code_r(numer, denom):
    mean = numer / jnp.maximum(denom, 1e-30)
    root = fourth_root(jnp.minimum(jnp.abs(mean) * (1.0 / W_MAX), 1.0))
    code = (root * R_TOP + 0.5).astype(I32)
    return jnp.where(mean < 0.0, -code, code).astype(I16)


def read_r(code):
    value = code.astype(F32)
    root = value * (1.0 / R_TOP)
    square = root * root
    return square * square * jnp.where(value < 0.0, -W_MAX, W_MAX)


def kernel(seq_ref, acts_hbm, cot_hbm, w_hbm, out_hbm,
           acts, xt, cot, w_own, w_rx, f32_f, sums, mine, x1s, x1r, x2s, x2r, zs, zr, out,
           load_sem, s_w, r_w, s_one, r_one, s_z, r_z, s_az, r_az, s_out):
    cols = cot.shape[1]
    groups = cols // LANES
    seq_count = seq_ref.shape[0]
    seq_len = cot.shape[0] // seq_count
    ck, tn = lax.axis_index("ckpt"), lax.axis_index("tensor")
    x, zh = ck // 4, ck % 4
    zl, y, core = tn // 8, (tn // 2) % 4, tn % 2
    xa, xb = ((x + 1) // 2) % 2, x // 2
    ya, yb = ((y + 1) // 2) % 2, y // 2
    to_zl = (ck, (1 - zl) * 8 + y * 2 + core)
    to_core = (ck, zl * 8 + y * 2 + 1 - core)
    to_y = [(ck, zl * 8 + (y + 1 - 2 * (y % 2)) * 2 + core), (ck, zl * 8 + (3 - y) * 2 + core)]
    to_x = [((x + 1 - 2 * (x % 2)) * 4 + zh, tn), ((3 - x) * 4 + zh, tn)]
    to_z = [(x * 4 + (zh + j) % 4, tn) for j in range(4)]
    bit = [xa, xb]
    ZL, Y1, Y2, CO, X1, X2, A1, A2 = range(8)

    barrier = pltpu.get_barrier_semaphore()
    others = [to_zl, to_core, *to_y, *to_x, *to_z[1:]]
    for other in others:
        pl.semaphore_signal(barrier, 1, device_id=other, device_id_type=MESH)

    load_acts = pltpu.make_async_copy(acts_hbm, acts, load_sem.at[0])
    load_cot = pltpu.make_async_copy(cot_hbm, cot, load_sem.at[1])
    load_w = pltpu.make_async_copy(w_hbm, w_own, load_sem.at[2])
    load_acts.start()
    load_cot.start()
    load_w.start()

    def rows(n, size):
        return pl.ds(pl.multiple_of(n * size, size), size)

    def remote(src, dst, send, recv, to):
        return pltpu.make_async_remote_copy(src, dst, send, recv, device_id=to, device_id_type=MESH)

    def one(stage, u, ref, to):
        return remote(ref, ref, s_one.at[stage, u], r_one.at[stage, u], to)

    def weights(par):
        return remote(w_hbm.at[:, par, rows(1 - bit[par], ROWS // 2)], w_rx.at[:, par],
                      s_w.at[par], r_w.at[par], to_x[par])

    def copy_zl(u, par):
        return one(ZL, u, xt.at[zl, yb, ya, core, u], to_zl)

    def copy_y1(u, par):
        return one(Y1, u, xt.at[:, yb, ya, core, u], to_y[par])

    def copy_y2(u, par):
        ref = xt.at[:, yb, :, core, u] if par == 0 else xt.at[:, :, ya, core, u]
        return one(Y2, u, ref, to_y[1 - par])

    def copy_core(u, par):
        return one(CO, u, xt.at[:, :, :, core, u], to_core)

    def copy_x1(u, par):
        return remote(x1s.at[u], x1r.at[u], s_one.at[X1, u], r_one.at[X1, u], to_x[par])

    def copy_x2(u, par):
        return remote(x2s.at[u], x2r.at[u], s_one.at[X2, u], r_one.at[X2, u], to_x[1 - par])

    def copy_z(u, j):
        return remote(zs.at[u, j - 1], zr.at[u, j - 1], s_z.at[u, j - 1], r_z.at[u, j - 1], to_z[j])

    def region(u, par, size):
        first, second = bit[par], bit[1 - par]
        if size == 128:
            return out.at[u, rows(first, 128)]
        if size == 64:
            return out.at[u, rows(first * 2 + second, 64)]
        return out.at[u, rows(first * 8 + second * 4 + zh, 16)]

    def copy_az(u, par, j):
        ref = region(u, par, 16)
        return remote(ref, ref, s_az.at[u, j - 1], r_az.at[u, j - 1], to_z[j])

    def copy_a1(u, par):
        return one(A1, u, region(u, par, 64), to_x[1 - par])

    def copy_a2(u, par):
        return one(A2, u, region(u, par, 128), to_x[par])

    def copy_out(u):
        return pltpu.make_async_copy(out.at[u], out_hbm.at[u], s_out.at[u])

    def turn(u):
        block = acts[:, pl.ds(pl.multiple_of(u * ROWS, ROWS), ROWS)]
        xt[zl, yb, ya, core, u] = block.astype(F32).T.astype(BF16)

    def do_turn(u, par):
        turn(u)
        copy_zl(u, par).start()

    def do_y1(u, par):
        copy_zl(u, par).wait_recv()
        copy_y1(u, par).start()

    def do_y2(u, par):
        copy_y1(u, par).wait_recv()
        copy_y2(u, par).start()

    def do_core(u, par):
        copy_y2(u, par).wait_recv()
        copy_core(u, par).start()

    def do_fisher(u, par):
        copy_core(u, par).wait_recv()
        slot = u % SLOTS
        total = None
        for seq in range(seq_count):
            near, far = seq // 2, seq % 2
            order = (0, 1) if far == 0 else (1, 0)
            left = jnp.concatenate(
                [xt[near, far, a, c, u] for a in order for c in range(2)], axis=1)
            grad = jnp.dot(left, cot[seq * seq_len:(seq + 1) * seq_len, :], preferred_element_type=F32)
            total = grad * grad if total is None else total + grad * grad
        f32_f[slot] = total
        most = total[:, :LANES]
        for g in range(1, groups):
            most = jnp.maximum(most, total[:, g * LANES:(g + 1) * LANES])
        top = most[:TILE]
        for r in range(1, ROWS // TILE):
            top = jnp.maximum(top, most[r * TILE:(r + 1) * TILE])
        exponent = jnp.ceil(jnp.log2(jnp.maximum(top, 1e-30)) + 0.01).astype(I32).astype(I16)
        count = ROWS // 2 // TILE
        x1s[u, count * groups] = exponent
        inverse = wide(1.0 / scale_of(exponent), groups)
        base = (1 - bit[par]) * count

        def step(r, carry):
            code = code_d(f32_f[slot, rows(base + r, TILE)], inverse)
            for g in range(groups):
                x1s[u, r * groups + g] = code[:, g * LANES:(g + 1) * LANES]
            return carry

        lax.fori_loop(0, count, step, 0)
        copy_x1(u, par).start()

    def tiles(ref, u, at):
        return jnp.concatenate([ref[u, at + g] for g in range(groups)], axis=1)

    def do_x2(u, par):
        copy_x1(u, par).wait_recv()
        slot = u % SLOTS
        count = ROWS // 2 // TILE
        half = count // 2
        e_own, e_rx = x1s[u, count * groups].astype(I32), x1r[u, count * groups].astype(I32)
        exponent = (jnp.maximum(e_own, e_rx) + 1).astype(I16)
        x2s[u, 2 * half * groups] = exponent
        inverse = wide(1.0 / scale_of(exponent), groups)
        scale = wide(scale_of(e_rx), groups)
        kept = bit[par] * count

        def both(r):
            f_own = f32_f[slot, rows(kept + r, TILE)]
            f_rx = read_d(tiles(x1r, u, r * groups), scale)
            own = w_own[u // 2, par, rows(kept + r, TILE)].astype(F32)
            other = w_rx[u // 2, par, rows(r, TILE)].astype(F32)
            return f_own + f_rx, f_own * own + f_rx * other

        def send(r, carry):
            denom, numer = both((1 - bit[1 - par]) * half + r)
            d, m = code_d(denom, inverse), code_r(numer, denom)
            for g in range(groups):
                x2s[u, r * groups + g] = d[:, g * LANES:(g + 1) * LANES]
                x2s[u, (half + r) * groups + g] = m[:, g * LANES:(g + 1) * LANES]
            return carry

        lax.fori_loop(0, half, send, 0)
        copy_x2(u, par).start()

        def keep(r, carry):
            denom, numer = both(bit[1 - par] * half + r)
            sums[slot, 0, rows(r, TILE)] = denom
            sums[slot, 1, rows(r, TILE)] = numer
            return carry

        lax.fori_loop(0, half, keep, 0)

    def do_z(u, par):
        copy_x2(u, par).wait_recv()
        slot = u % SLOTS
        half = ROWS // 4 // TILE
        e_own, e_rx = x2s[u, 2 * half * groups].astype(I32), x2r[u, 2 * half * groups].astype(I32)
        exponent = (jnp.maximum(e_own, e_rx) + 1).astype(I16)
        inverse = wide(1.0 / scale_of(exponent), groups)
        scale = wide(scale_of(e_rx), groups)
        for j in (1, 2, 3, 0):
            at = (zh + j) % 4
            d_rx = read_d(tiles(x2r, u, at * groups), scale)
            denom = sums[slot, 0, rows(at, TILE)] + d_rx
            numer = sums[slot, 1, rows(at, TILE)] + d_rx * read_r(tiles(x2r, u, (half + at) * groups))
            if j == 0:
                mine[slot, 0] = denom
                mine[slot, 1] = numer
                continue
            d, m = code_d(denom, inverse), code_r(numer, denom)
            for g in range(groups):
                zs[u, j - 1, g] = d[:, g * LANES:(g + 1) * LANES]
                zs[u, j - 1, groups + g] = m[:, g * LANES:(g + 1) * LANES]
            zs[u, j - 1, 2 * groups] = exponent
            copy_z(u, j).start()

    def do_merge(u, par):
        slot = u % SLOTS
        denom, numer = mine[slot, 0], mine[slot, 1]
        for j in (1, 2, 3):
            copy_z(u, j).wait_recv()
            scale = wide(scale_of(zr[u, j - 1, 2 * groups].astype(I32)), groups)
            d_rx = read_d(jnp.concatenate([zr[u, j - 1, g] for g in range(groups)], axis=1), scale)
            m_rx = read_r(jnp.concatenate([zr[u, j - 1, groups + g] for g in range(groups)], axis=1))
            denom = denom + d_rx
            numer = numer + d_rx * m_rx
        region(u, par, 16)[...] = (numer / (denom + 1e-6)).astype(BF16)
        for j in (1, 2, 3):
            copy_az(u, par, j).start()

    def do_a1(u, par):
        for j in (1, 2, 3):
            copy_az(u, par, j).wait_recv()
        copy_a1(u, par).start()

    def do_a2(u, par):
        copy_a1(u, par).wait_recv()
        copy_a2(u, par).start()

    def do_out(u, par):
        copy_a2(u, par).wait_recv()
        copy_out(u).start()

    load_acts.wait()
    pl.semaphore_wait(barrier, len(others))
    for par in range(2):
        weights(par).start()

    load_cot.wait()

    def mask(b, carry):
        size = 64
        seq = b // (seq_len // size)
        at = (b % (seq_len // size)) * size
        block = cot[rows(b, size)].astype(F32)
        position = lax.broadcasted_iota(I32, (size, cols), 0) + at
        cot[rows(b, size)] = jnp.where(position < seq_ref[seq], block, 0.0).astype(BF16)
        return carry

    def prepare(b):
        lax.fori_loop(0, cot.shape[0] // 64, mask, 0)
        load_w.wait()
        for par in range(2):
            weights(par).wait_recv()

    stages = [(do_out, 10), (do_a2, 9), (do_a1, 8), (do_merge, 7), (do_z, 6), (do_x2, 5),
              (do_fisher, 4), (do_core, 3), (do_y2, 2), (do_y1, 1), (do_turn, 0)]

    def pair(p, carry):
        for par in range(2):
            for stage, lag in stages:
                u = p * 2 + (par - lag)
                sort = (par - lag) % 2

                @pl.when(jnp.logical_and(u >= 0, u < UNITS))
                def _(stage=stage, u=u, sort=sort):
                    stage(u, sort)
            if par == 1:
                @pl.when(p == 1)
                def _():
                    prepare(0)
        return carry

    lax.fori_loop(0, (UNITS + 10) // 2, pair, 0)

    for par in range(2):
        weights(par).wait_send()

    def settle(p, carry):
        for par in range(2):
            u = p * 2 + par
            for copy in (copy_zl, copy_y1, copy_y2, copy_core, copy_x1, copy_x2, copy_a1, copy_a2):
                copy(u, par).wait_send()
            for j in (1, 2, 3):
                copy_z(u, j).wait_send()
                copy_az(u, par, j).wait_send()
            copy_out(u).wait()
        return carry

    lax.fori_loop(0, UNITS // 2, settle, 0)


def body(acts, cotangent, seq_lengths, up_weight):
    tokens, cols = cotangent.shape[1:]
    width = acts.shape[2]
    groups = cols // LANES
    any_space = pl.BlockSpec(memory_space=pl.ANY)
    half, quarter = ROWS // 2 // TILE, ROWS // 4 // TILE
    merged = pl.pallas_call(
        kernel,
        out_shape=jax.ShapeDtypeStruct((UNITS, ROWS, cols), BF16),
        in_specs=[pl.BlockSpec(memory_space=pltpu.SMEM), any_space, any_space, any_space],
        out_specs=any_space,
        scratch_shapes=[
            pltpu.VMEM((acts.shape[1], width), BF16),
            pltpu.VMEM((2, 2, 2, 2, UNITS, ROWS, LANES), BF16),
            pltpu.VMEM((tokens, cols), BF16),
            pltpu.VMEM((UNITS // 2, 2, ROWS, cols), BF16),
            pltpu.VMEM((UNITS // 2, 2, ROWS // 2, cols), BF16),
            pltpu.VMEM((SLOTS, ROWS, cols), F32),
            pltpu.VMEM((SLOTS, 2, ROWS // 4, cols), F32),
            pltpu.VMEM((SLOTS, 2, TILE, cols), F32),
            pltpu.VMEM((UNITS, half * groups + 1, TILE, LANES), I16),
            pltpu.VMEM((UNITS, half * groups + 1, TILE, LANES), I16),
            pltpu.VMEM((UNITS, 2 * quarter * groups + 1, TILE, LANES), I16),
            pltpu.VMEM((UNITS, 2 * quarter * groups + 1, TILE, LANES), I16),
            pltpu.VMEM((UNITS, 3, 2 * groups + 1, TILE, LANES), I16),
            pltpu.VMEM((UNITS, 3, 2 * groups + 1, TILE, LANES), I16),
            pltpu.VMEM((UNITS, ROWS, cols), BF16),
            pltpu.SemaphoreType.DMA((3,)),
            pltpu.SemaphoreType.DMA((2,)),
            pltpu.SemaphoreType.DMA((2,)),
            pltpu.SemaphoreType.DMA((8, UNITS)),
            pltpu.SemaphoreType.DMA((8, UNITS)),
            pltpu.SemaphoreType.DMA((UNITS, 3)),
            pltpu.SemaphoreType.DMA((UNITS, 3)),
            pltpu.SemaphoreType.DMA((UNITS, 3)),
            pltpu.SemaphoreType.DMA((UNITS, 3)),
            pltpu.SemaphoreType.DMA((UNITS,)),
        ],
        compiler_params=pltpu.CompilerParams(
            collective_id=0, has_side_effects=True, vmem_limit_bytes=58 * 2**20),
    )(seq_lengths, acts[0], cotangent[0], up_weight[0].reshape(UNITS // 2, 2, ROWS, cols))
    return merged.reshape(width, cols)


def solution(mesh):
    in_specs = (
        P("ckpt", "tensor", None),
        P("ckpt", None, "tensor"),
        P(),
        P("ckpt", None, "tensor"),
    )
    out_specs = P(None, "tensor")
    return jax.shard_map(body, mesh=mesh, in_specs=in_specs, out_specs=out_specs, check_vma=False)
```

```python
import jax
import jax.numpy as jnp
from jax import lax
from jax.experimental import pallas as pl
from jax.experimental.pallas import tpu as pltpu
from jax.sharding import PartitionSpec as P

MESH = pl.DeviceIdType.MESH
ORDER = (
    0, 1, 2, 3, 4, 14, 15, 5, 6, 16, 17, 7, 8, 28, 9, 29,
    18, 30, 31, 10, 42, 19, 20, 43, 11, 12, 56, 32, 13, 57, 44, 58,
    70, 45, 21, 33, 71, 34, 59, 72, 84, 22, 46, 85, 73, 60, 35, 47,
    23, 86, 61, 98, 48, 24, 87, 36, 62, 74, 99, 49, 37, 63, 25, 100,
    75, 76, 88, 26, 50, 38, 27, 101, 64, 77, 112, 51, 39, 89, 113, 65,
    114, 90, 115, 40, 52, 102, 66, 41, 103, 78, 126, 53, 91, 67, 104, 79,
    127, 92, 54, 80, 81, 105, 68, 55, 116, 117, 93, 128, 106, 69, 94, 82,
    129, 107, 140, 95, 141, 83, 118, 119, 96, 120, 130, 131, 142, 121, 97, 132,
    108, 143, 109, 133, 144, 110, 134, 135, 145, 111, 122, 123, 146, 147, 124, 125,
    148, 136, 137, 138, 139, 149, 150, 151, 152, 153,
)
F32, BF16, I16, I32 = jnp.float32, jnp.bfloat16, jnp.int16, jnp.int32
UNITS = 14
ROWS = 256
LANES = 128
TILE = 16
SLOTS = 14
D_TOP = 65504.0
D_MID = 32752
R_TOP = 32704.0
W_MAX = 0.125


def fourth_root(v):
    return jnp.sqrt(jnp.sqrt(v))


def wide(tile, count):
    return jnp.concatenate([tile] * count, axis=1)


def scale_of(exponent):
    return jnp.exp2(exponent.astype(F32))


def code_d(v, inverse):
    root = fourth_root(v * inverse)
    code = (root * D_TOP + 0.5).astype(I32) - D_MID
    return jnp.minimum(code, 32767).astype(I16)


def read_d(code, scale):
    root = (code.astype(F32) + float(D_MID)) * (1.0 / D_TOP)
    square = root * root
    return square * square * scale


def code_r(numer, denom):
    mean = numer / jnp.maximum(denom, 1e-30)
    root = fourth_root(jnp.minimum(jnp.abs(mean) * (1.0 / W_MAX), 1.0))
    code = (root * R_TOP + 0.5).astype(I32)
    return jnp.where(mean < 0.0, -code, code).astype(I16)


def read_r(code):
    value = code.astype(F32)
    root = value * (1.0 / R_TOP)
    square = root * root
    return square * square * jnp.where(value < 0.0, -W_MAX, W_MAX)


def kernel(seq_ref, acts_hbm, cot_hbm, w_hbm, out_hbm,
           acts, xt, cot, w_own, w_rx, f32_f, sums, mine, x1s, x1r, x2s, x2r, zs, zr, out,
           load_sem, s_w, r_w, s_one, r_one, s_z, r_z, s_az, r_az, s_out):
    cols = cot.shape[1]
    groups = cols // LANES
    seq_count = seq_ref.shape[0]
    seq_len = cot.shape[0] // seq_count
    ck, tn = lax.axis_index("ckpt"), lax.axis_index("tensor")
    x, zh = ck // 4, ck % 4
    zl, y, core = tn // 8, (tn // 2) % 4, tn % 2
    xa, xb = ((x + 1) // 2) % 2, x // 2
    ya, yb = ((y + 1) // 2) % 2, y // 2
    to_zl = (ck, (1 - zl) * 8 + y * 2 + core)
    to_core = (ck, zl * 8 + y * 2 + 1 - core)
    to_y = [(ck, zl * 8 + (y + 1 - 2 * (y % 2)) * 2 + core), (ck, zl * 8 + (3 - y) * 2 + core)]
    to_x = [((x + 1 - 2 * (x % 2)) * 4 + zh, tn), ((3 - x) * 4 + zh, tn)]
    to_z = [(x * 4 + (zh + j) % 4, tn) for j in range(4)]
    bit = [xa, xb]
    ZL, Y1, Y2, CO, X1, X2, A1, A2 = range(8)

    barrier = pltpu.get_barrier_semaphore()
    others = [to_zl, to_core, *to_y, *to_x, *to_z[1:]]
    for other in others:
        pl.semaphore_signal(barrier, 1, device_id=other, device_id_type=MESH)

    load_acts = pltpu.make_async_copy(acts_hbm, acts, load_sem.at[0])
    load_cot = pltpu.make_async_copy(cot_hbm, cot, load_sem.at[1])
    load_w = pltpu.make_async_copy(w_hbm, w_own, load_sem.at[2])
    load_acts.start()
    load_cot.start()
    load_w.start()

    def rows(n, size):
        return pl.ds(pl.multiple_of(n * size, size), size)

    def remote(src, dst, send, recv, to):
        return pltpu.make_async_remote_copy(src, dst, send, recv, device_id=to, device_id_type=MESH)

    def one(stage, u, ref, to):
        return remote(ref, ref, s_one.at[stage, u], r_one.at[stage, u], to)

    def weights(par):
        return remote(w_hbm.at[:, par, rows(1 - bit[par], ROWS // 2)], w_rx.at[:, par],
                      s_w.at[par], r_w.at[par], to_x[par])

    def copy_zl(u, par):
        return one(ZL, u, xt.at[zl, yb, ya, core, u], to_zl)

    def copy_y1(u, par):
        return one(Y1, u, xt.at[:, yb, ya, core, u], to_y[par])

    def copy_y2(u, par):
        ref = xt.at[:, yb, :, core, u] if par == 0 else xt.at[:, :, ya, core, u]
        return one(Y2, u, ref, to_y[1 - par])

    def copy_core(u, par):
        return one(CO, u, xt.at[:, :, :, core, u], to_core)

    def copy_x1(u, par):
        return remote(x1s.at[u], x1r.at[u], s_one.at[X1, u], r_one.at[X1, u], to_x[par])

    def copy_x2(u, par):
        return remote(x2s.at[u], x2r.at[u], s_one.at[X2, u], r_one.at[X2, u], to_x[1 - par])

    def copy_z(u, j):
        return remote(zs.at[u, j - 1], zr.at[u, j - 1], s_z.at[u, j - 1], r_z.at[u, j - 1], to_z[j])

    def region(u, par, size):
        first, second = bit[par], bit[1 - par]
        if size == 128:
            return out.at[u, rows(first, 128)]
        if size == 64:
            return out.at[u, rows(first * 2 + second, 64)]
        return out.at[u, rows(first * 8 + second * 4 + zh, 16)]

    def copy_az(u, par, j):
        ref = region(u, par, 16)
        return remote(ref, ref, s_az.at[u, j - 1], r_az.at[u, j - 1], to_z[j])

    def copy_a1(u, par):
        return one(A1, u, region(u, par, 64), to_x[1 - par])

    def copy_a2(u, par):
        return one(A2, u, region(u, par, 128), to_x[par])

    def copy_out(u):
        return pltpu.make_async_copy(out.at[u], out_hbm.at[u], s_out.at[u])

    def turn(u):
        block = acts[:, pl.ds(pl.multiple_of(u * ROWS, ROWS), ROWS)]
        xt[zl, yb, ya, core, u] = block.astype(F32).T.astype(BF16)

    def mask(b, carry):
        size = 64
        seq = b // (seq_len // size)
        at = (b % (seq_len // size)) * size
        block = cot[rows(b, size)].astype(F32)
        position = lax.broadcasted_iota(I32, (size, cols), 0) + at
        cot[rows(b, size)] = jnp.where(position < seq_ref[seq], block, 0.0).astype(BF16)
        return carry

    def do_turn(u, par):
        turn(u)
        copy_zl(u, par).start()

    def do_y1(u, par):
        copy_zl(u, par).wait_recv()
        copy_y1(u, par).start()

    def do_y2(u, par):
        copy_y1(u, par).wait_recv()
        copy_y2(u, par).start()

    def do_core(u, par):
        copy_y2(u, par).wait_recv()
        copy_core(u, par).start()

    def do_fisher(u, par):
        copy_core(u, par).wait_recv()
        if u == 0:
            load_cot.wait()
            lax.fori_loop(0, cot.shape[0] // 64, mask, 0)
        slot = u % SLOTS
        total = None
        for seq in range(seq_count):
            near, far = seq // 2, seq % 2
            order = (0, 1) if far == 0 else (1, 0)
            left = jnp.concatenate(
                [xt[near, far, a, c, u] for a in order for c in range(2)], axis=1)
            grad = jnp.dot(left, cot[seq * seq_len:(seq + 1) * seq_len, :], preferred_element_type=F32)
            total = grad * grad if total is None else total + grad * grad
        f32_f[slot] = total
        most = total[:, :LANES]
        for g in range(1, groups):
            most = jnp.maximum(most, total[:, g * LANES:(g + 1) * LANES])
        top = most[:TILE]
        for r in range(1, ROWS // TILE):
            top = jnp.maximum(top, most[r * TILE:(r + 1) * TILE])
        exponent = jnp.ceil(jnp.log2(jnp.maximum(top, 1e-30)) + 0.01).astype(I32).astype(I16)
        count = ROWS // 2 // TILE
        x1s[u, count * groups] = exponent
        inverse = wide(1.0 / scale_of(exponent), groups)
        base = (1 - bit[par]) * count

        def step(r, carry):
            code = code_d(f32_f[slot, rows(base + r, TILE)], inverse)
            for g in range(groups):
                x1s[u, r * groups + g] = code[:, g * LANES:(g + 1) * LANES]
            return carry

        lax.fori_loop(0, count, step, 0)
        copy_x1(u, par).start()

    def tiles(ref, u, at):
        return jnp.concatenate([ref[u, at + g] for g in range(groups)], axis=1)

    def do_x2(u, par):
        copy_x1(u, par).wait_recv()
        if u == 0:
            load_w.wait()
            for sort in range(2):
                weights(sort).wait_recv()
        slot = u % SLOTS
        count = ROWS // 2 // TILE
        half = count // 2
        e_own, e_rx = x1s[u, count * groups].astype(I32), x1r[u, count * groups].astype(I32)
        exponent = (jnp.maximum(e_own, e_rx) + 1).astype(I16)
        x2s[u, 2 * half * groups] = exponent
        inverse = wide(1.0 / scale_of(exponent), groups)
        scale = wide(scale_of(e_rx), groups)
        kept = bit[par] * count

        def both(r):
            f_own = f32_f[slot, rows(kept + r, TILE)]
            f_rx = read_d(tiles(x1r, u, r * groups), scale)
            own = w_own[u // 2, par, rows(kept + r, TILE)].astype(F32)
            other = w_rx[u // 2, par, rows(r, TILE)].astype(F32)
            return f_own + f_rx, f_own * own + f_rx * other

        def send(r, carry):
            denom, numer = both((1 - bit[1 - par]) * half + r)
            d, m = code_d(denom, inverse), code_r(numer, denom)
            for g in range(groups):
                x2s[u, r * groups + g] = d[:, g * LANES:(g + 1) * LANES]
                x2s[u, (half + r) * groups + g] = m[:, g * LANES:(g + 1) * LANES]
            return carry

        lax.fori_loop(0, half, send, 0)
        copy_x2(u, par).start()

        def keep(r, carry):
            denom, numer = both(bit[1 - par] * half + r)
            sums[slot, 0, rows(r, TILE)] = denom
            sums[slot, 1, rows(r, TILE)] = numer
            return carry

        lax.fori_loop(0, half, keep, 0)

    def do_z(u, par):
        copy_x2(u, par).wait_recv()
        slot = u % SLOTS
        half = ROWS // 4 // TILE
        e_own, e_rx = x2s[u, 2 * half * groups].astype(I32), x2r[u, 2 * half * groups].astype(I32)
        exponent = (jnp.maximum(e_own, e_rx) + 1).astype(I16)
        inverse = wide(1.0 / scale_of(exponent), groups)
        scale = wide(scale_of(e_rx), groups)
        for j in (1, 2, 3, 0):
            at = (zh + j) % 4
            d_rx = read_d(tiles(x2r, u, at * groups), scale)
            denom = sums[slot, 0, rows(at, TILE)] + d_rx
            numer = sums[slot, 1, rows(at, TILE)] + d_rx * read_r(tiles(x2r, u, (half + at) * groups))
            if j == 0:
                mine[slot, 0] = denom
                mine[slot, 1] = numer
                continue
            d, m = code_d(denom, inverse), code_r(numer, denom)
            for g in range(groups):
                zs[u, j - 1, g] = d[:, g * LANES:(g + 1) * LANES]
                zs[u, j - 1, groups + g] = m[:, g * LANES:(g + 1) * LANES]
            zs[u, j - 1, 2 * groups] = exponent
            copy_z(u, j).start()

    def do_merge(u, par):
        slot = u % SLOTS
        denom, numer = mine[slot, 0], mine[slot, 1]
        for j in (1, 2, 3):
            copy_z(u, j).wait_recv()
            scale = wide(scale_of(zr[u, j - 1, 2 * groups].astype(I32)), groups)
            d_rx = read_d(jnp.concatenate([zr[u, j - 1, g] for g in range(groups)], axis=1), scale)
            m_rx = read_r(jnp.concatenate([zr[u, j - 1, groups + g] for g in range(groups)], axis=1))
            denom = denom + d_rx
            numer = numer + d_rx * m_rx
        region(u, par, 16)[...] = (numer / (denom + 1e-6)).astype(BF16)
        for j in (1, 2, 3):
            copy_az(u, par, j).start()

    def do_a1(u, par):
        for j in (1, 2, 3):
            copy_az(u, par, j).wait_recv()
        copy_a1(u, par).start()

    def do_a2(u, par):
        copy_a1(u, par).wait_recv()
        copy_a2(u, par).start()

    def do_out(u, par):
        copy_a2(u, par).wait_recv()
        copy_out(u).start()

    load_acts.wait()
    pl.semaphore_wait(barrier, len(others))
    for par in range(2):
        weights(par).start()

    stages = (do_turn, do_y1, do_y2, do_core, do_fisher, do_x2, do_z, do_merge, do_a1, do_a2, do_out)
    for step in ORDER:
        stages[step // UNITS](step % UNITS, step % UNITS % 2)

    for par in range(2):
        weights(par).wait_send()

    def settle(p, carry):
        for par in range(2):
            u = p * 2 + par
            for copy in (copy_zl, copy_y1, copy_y2, copy_core, copy_x1, copy_x2, copy_a1, copy_a2):
                copy(u, par).wait_send()
            for j in (1, 2, 3):
                copy_z(u, j).wait_send()
                copy_az(u, par, j).wait_send()
            copy_out(u).wait()
        return carry

    lax.fori_loop(0, UNITS // 2, settle, 0)


def body(acts, cotangent, seq_lengths, up_weight):
    tokens, cols = cotangent.shape[1:]
    width = acts.shape[2]
    groups = cols // LANES
    any_space = pl.BlockSpec(memory_space=pl.ANY)
    half, quarter = ROWS // 2 // TILE, ROWS // 4 // TILE
    merged = pl.pallas_call(
        kernel,
        out_shape=jax.ShapeDtypeStruct((UNITS, ROWS, cols), BF16),
        in_specs=[pl.BlockSpec(memory_space=pltpu.SMEM), any_space, any_space, any_space],
        out_specs=any_space,
        scratch_shapes=[
            pltpu.VMEM((acts.shape[1], width), BF16),
            pltpu.VMEM((2, 2, 2, 2, UNITS, ROWS, LANES), BF16),
            pltpu.VMEM((tokens, cols), BF16),
            pltpu.VMEM((UNITS // 2, 2, ROWS, cols), BF16),
            pltpu.VMEM((UNITS // 2, 2, ROWS // 2, cols), BF16),
            pltpu.VMEM((SLOTS, ROWS, cols), F32),
            pltpu.VMEM((SLOTS, 2, ROWS // 4, cols), F32),
            pltpu.VMEM((SLOTS, 2, TILE, cols), F32),
            pltpu.VMEM((UNITS, half * groups + 1, TILE, LANES), I16),
            pltpu.VMEM((UNITS, half * groups + 1, TILE, LANES), I16),
            pltpu.VMEM((UNITS, 2 * quarter * groups + 1, TILE, LANES), I16),
            pltpu.VMEM((UNITS, 2 * quarter * groups + 1, TILE, LANES), I16),
            pltpu.VMEM((UNITS, 3, 2 * groups + 1, TILE, LANES), I16),
            pltpu.VMEM((UNITS, 3, 2 * groups + 1, TILE, LANES), I16),
            pltpu.VMEM((UNITS, ROWS, cols), BF16),
            pltpu.SemaphoreType.DMA((3,)),
            pltpu.SemaphoreType.DMA((2,)),
            pltpu.SemaphoreType.DMA((2,)),
            pltpu.SemaphoreType.DMA((8, UNITS)),
            pltpu.SemaphoreType.DMA((8, UNITS)),
            pltpu.SemaphoreType.DMA((UNITS, 3)),
            pltpu.SemaphoreType.DMA((UNITS, 3)),
            pltpu.SemaphoreType.DMA((UNITS, 3)),
            pltpu.SemaphoreType.DMA((UNITS, 3)),
            pltpu.SemaphoreType.DMA((UNITS,)),
        ],
        compiler_params=pltpu.CompilerParams(
            collective_id=0, has_side_effects=True, vmem_limit_bytes=58 * 2**20),
    )(seq_lengths, acts[0], cotangent[0], up_weight[0].reshape(UNITS // 2, 2, ROWS, cols))
    return merged.reshape(width, cols)


def solution(mesh):
    in_specs = (
        P("ckpt", "tensor", None),
        P("ckpt", None, "tensor"),
        P(),
        P("ckpt", None, "tensor"),
    )
    out_specs = P(None, "tensor")
    return jax.shard_map(body, mesh=mesh, in_specs=in_specs, out_specs=out_specs, check_vma=False)
```

```python
import jax
import jax.numpy as jnp
from jax import lax
from jax.experimental import pallas as pl
from jax.experimental.pallas import tpu as pltpu
from jax.sharding import PartitionSpec as P

MESH = pl.DeviceIdType.MESH
LATE_ZL = (0,)
TREE_Z = (0, 1, 2, 3, 4, 5, 6, 7, 8, 9)
TREE_B = ()
DIRECT_X = (12, 13)
ORDER = (
    0, 1, 2, 3, 4, 5, 14, 6, 15, 16, 17, 18, 28, 7, 8, 19,
    29, 30, 31, 42, 32, 20, 43, 21, 56, 57, 9, 33, 22, 44, 58, 70,
    45, 23, 71, 46, 34, 35, 10, 59, 11, 60, 72, 84, 47, 24, 36, 85,
    73, 37, 12, 61, 25, 13, 48, 86, 98, 74, 62, 49, 87, 75, 99, 63,
    112, 100, 126, 50, 88, 38, 76, 113, 64, 39, 89, 51, 140, 127, 101, 77,
    114, 128, 26, 65, 102, 90, 78, 154, 27, 52, 115, 91, 66, 103, 53, 79,
    40, 41, 129, 141, 142, 168, 104, 116, 67, 92, 117, 80, 143, 118, 93, 81,
    130, 144, 105, 54, 106, 155, 131, 156, 94, 157, 55, 132, 68, 107, 69, 119,
    145, 169, 95, 158, 120, 170, 133, 108, 134, 171, 121, 109, 135, 146, 82, 147,
    83, 159, 160, 122, 172, 123, 136, 96, 148, 161, 149, 173, 97, 150, 137, 151,
    110, 162, 174, 111, 163, 175, 124, 138, 164, 165, 125, 176, 139, 177, 152, 178,
    179, 166, 153, 167, 180, 181,
)
F32, BF16, I16, I32 = jnp.float32, jnp.bfloat16, jnp.int16, jnp.int32
UNITS = 14
ROWS = 256
LANES = 128
TILE = 16
SLOTS = 14
D_TOP = 65504.0
D_MID = 32752
R_TOP = 32704.0
W_MAX = 0.125


def fourth_root(v):
    return jnp.sqrt(jnp.sqrt(v))


def wide(tile, count):
    return jnp.concatenate([tile] * count, axis=1)


def scale_of(exponent):
    return jnp.exp2(exponent.astype(F32))


def code_d(v, inverse):
    root = fourth_root(v * inverse)
    code = (root * D_TOP + 0.5).astype(I32) - D_MID
    return jnp.minimum(code, 32767).astype(I16)


def read_d(code, scale):
    root = (code.astype(F32) + float(D_MID)) * (1.0 / D_TOP)
    square = root * root
    return square * square * scale


def code_r(numer, denom):
    mean = numer / jnp.maximum(denom, 1e-30)
    root = fourth_root(jnp.minimum(jnp.abs(mean) * (1.0 / W_MAX), 1.0))
    code = (root * R_TOP + 0.5).astype(I32)
    return jnp.where(mean < 0.0, -code, code).astype(I16)


def read_r(code):
    value = code.astype(F32)
    root = value * (1.0 / R_TOP)
    square = root * root
    return square * square * jnp.where(value < 0.0, -W_MAX, W_MAX)


def kernel(seq_ref, acts_hbm, cot_hbm, w_hbm, out_hbm,
           acts, xt, cot, w_own, w_rx, f32_f, sums, sums2, mine,
           x1s, x1r, x2s, x2r, zas, zar, zs, zr, out,
           load_sem, s_w, r_w, s_one, r_one, s_z, r_z, s_az, r_az, s_ad, r_ad, s_out):
    cols = cot.shape[1]
    groups = cols // LANES
    seq_count = seq_ref.shape[0]
    seq_len = cot.shape[0] // seq_count
    ck, tn = lax.axis_index("ckpt"), lax.axis_index("tensor")
    x, zh = ck // 4, ck % 4
    zl, y, core = tn // 8, (tn // 2) % 4, tn % 2
    xa, xb = ((x + 1) // 2) % 2, x // 2
    ya, yb = ((y + 1) // 2) % 2, y // 2
    to_zl = (ck, (1 - zl) * 8 + y * 2 + core)
    to_core = (ck, zl * 8 + y * 2 + 1 - core)
    to_y = [(ck, zl * 8 + (y + 1 - 2 * (y % 2)) * 2 + core), (ck, zl * 8 + (3 - y) * 2 + core)]
    to_x = [((x + 1 - 2 * (x % 2)) * 4 + zh, tn), ((3 - x) * 4 + zh, tn)]
    to_far_x = ((x + 2) % 4 * 4 + zh, tn)
    to_z = [(x * 4 + (zh + j) % 4, tn) for j in range(4)]
    to_zp = [(x * 4 + zh + 1 - 2 * (zh % 2), tn), (x * 4 + 3 - zh, tn)]
    bit = [xa, xb]

    def z_bits(n):
        return [((n + 1) // 2) % 2, n // 2]

    def group(n, par):
        bits = z_bits(n)
        return bits[par] * 2 + bits[1 - par]

    z_bit = z_bits(zh)
    ZL, Y0, Y1, Y2, CO, X1, X2, ZA, B1, B2, A1, A2 = range(12)

    barrier = pltpu.get_barrier_semaphore()
    others = [to_zl, to_core, *to_y, *to_x, to_far_x, *to_z[1:]]
    for other in others:
        pl.semaphore_signal(barrier, 1, device_id=other, device_id_type=MESH)

    load_acts = pltpu.make_async_copy(acts_hbm, acts, load_sem.at[0])
    load_cot = pltpu.make_async_copy(cot_hbm, cot, load_sem.at[1])
    load_w = pltpu.make_async_copy(w_hbm, w_own, load_sem.at[2])
    load_acts.start()
    load_cot.start()
    load_w.start()

    def rows(n, size):
        return pl.ds(pl.multiple_of(n * size, size), size)

    def remote(src, dst, send, recv, to):
        return pltpu.make_async_remote_copy(src, dst, send, recv, device_id=to, device_id_type=MESH)

    def one(stage, u, ref, to):
        return remote(ref, ref, s_one.at[stage, u], r_one.at[stage, u], to)

    def weights(par):
        return remote(w_hbm.at[:, par, rows(1 - bit[par], ROWS // 2)], w_rx.at[:, par],
                      s_w.at[par], r_w.at[par], to_x[par])

    def copy_zl(u, par):
        ref = xt.at[zl, :, :, core, u] if u in LATE_ZL else xt.at[zl, yb, ya, core, u]
        return one(ZL, u, ref, to_zl)

    def copy_y0(u, par):
        return one(Y0, u, xt.at[zl, yb, ya, core, u], to_y[par])

    def copy_y1(u, par):
        return one(Y1, u, xt.at[1 - zl, yb, ya, core, u], to_y[par])

    def copy_y2(u, par):
        layer = zl if u in LATE_ZL else slice(None)
        ref = xt.at[layer, yb, :, core, u] if par == 0 else xt.at[layer, :, ya, core, u]
        return one(Y2, u, ref, to_y[1 - par])

    def copy_core(u, par):
        return one(CO, u, xt.at[:, :, :, core, u], to_core)

    def copy_x1(u, par):
        return remote(x1s.at[u], x1r.at[u], s_one.at[X1, u], r_one.at[X1, u], to_x[par])

    def copy_x2(u, par):
        return remote(x2s.at[u], x2r.at[u], s_one.at[X2, u], r_one.at[X2, u], to_x[1 - par])

    def copy_z(u, j):
        return remote(zs.at[u, j - 1], zr.at[u, j - 1], s_z.at[u, j - 1], r_z.at[u, j - 1], to_z[j])

    def region(u, par, size):
        first, second = bit[par], bit[1 - par]
        if size == 128:
            return out.at[u, rows(first, 128)]
        if size == 64:
            return out.at[u, rows(first * 2 + second, 64)]
        if size == 32:
            return out.at[u, rows(first * 4 + second * 2 + z_bit[par], 32)]
        return out.at[u, rows(first * 8 + second * 4 + group(zh, par), 16)]

    def copy_za(u, par):
        return remote(zas.at[u], zar.at[u], s_one.at[ZA, u], r_one.at[ZA, u], to_zp[par])

    def copy_zb(u, par):
        return remote(zs.at[u, 0], zr.at[u, 0], s_z.at[u, 0], r_z.at[u, 0], to_zp[1 - par])

    def copy_b1(u, par):
        return one(B1, u, region(u, par, 16), to_zp[1 - par])

    def copy_b2(u, par):
        return one(B2, u, region(u, par, 32), to_zp[par])

    def copies_ad(u, par):
        ref = region(u, par, 64)
        return [remote(ref, ref, s_ad.at[u, k], r_ad.at[u, k], to)
                for k, to in enumerate((*to_x, to_far_x))]

    def copy_az(u, par, j):
        ref = region(u, par, 16)
        return remote(ref, ref, s_az.at[u, j - 1], r_az.at[u, j - 1], to_z[j])

    def copy_a1(u, par):
        return one(A1, u, region(u, par, 64), to_x[1 - par])

    def copy_a2(u, par):
        return one(A2, u, region(u, par, 128), to_x[par])

    def copy_out(u):
        return pltpu.make_async_copy(out.at[u], out_hbm.at[u], s_out.at[u])

    def turn(u):
        block = acts[:, pl.ds(pl.multiple_of(u * ROWS, ROWS), ROWS)]
        xt[zl, yb, ya, core, u] = block.astype(F32).T.astype(BF16)

    def mask(b, carry):
        size = 64
        seq = b // (seq_len // size)
        at = (b % (seq_len // size)) * size
        block = cot[rows(b, size)].astype(F32)
        position = lax.broadcasted_iota(I32, (size, cols), 0) + at
        cot[rows(b, size)] = jnp.where(position < seq_ref[seq], block, 0.0).astype(BF16)
        return carry

    def do_turn(u, par):
        turn(u)
        if u not in LATE_ZL:
            copy_zl(u, par).start()
        copy_y0(u, par).start()

    def do_y1(u, par):
        if u in LATE_ZL:
            copy_y0(u, par).wait_recv()
            copy_y2(u, par).start()
        else:
            copy_zl(u, par).wait_recv()
            copy_y1(u, par).start()

    def do_y2(u, par):
        if u in LATE_ZL:
            copy_y2(u, par).wait_recv()
            copy_zl(u, par).start()
        else:
            copy_y0(u, par).wait_recv()
            copy_y1(u, par).wait_recv()
            copy_y2(u, par).start()

    def do_core(u, par):
        (copy_zl if u in LATE_ZL else copy_y2)(u, par).wait_recv()
        copy_core(u, par).start()

    def do_fisher(u, par):
        copy_core(u, par).wait_recv()
        if u == 0:
            load_cot.wait()
            lax.fori_loop(0, cot.shape[0] // 64, mask, 0)
        slot = u % SLOTS
        total = None
        for seq in range(seq_count):
            near, far = seq // 2, seq % 2
            order = (0, 1) if far == 0 else (1, 0)
            left = jnp.concatenate(
                [xt[near, far, a, c, u] for a in order for c in range(2)], axis=1)
            grad = jnp.dot(left, cot[seq * seq_len:(seq + 1) * seq_len, :], preferred_element_type=F32)
            total = grad * grad if total is None else total + grad * grad
        f32_f[slot] = total
        most = total[:, :LANES]
        for g in range(1, groups):
            most = jnp.maximum(most, total[:, g * LANES:(g + 1) * LANES])
        top = most[:TILE]
        for r in range(1, ROWS // TILE):
            top = jnp.maximum(top, most[r * TILE:(r + 1) * TILE])
        exponent = jnp.ceil(jnp.log2(jnp.maximum(top, 1e-30)) + 0.01).astype(I32).astype(I16)
        count = ROWS // 2 // TILE
        x1s[u, count * groups] = exponent
        inverse = wide(1.0 / scale_of(exponent), groups)
        base = (1 - bit[par]) * count

        def step(r, carry):
            code = code_d(f32_f[slot, rows(base + r, TILE)], inverse)
            for g in range(groups):
                x1s[u, r * groups + g] = code[:, g * LANES:(g + 1) * LANES]
            return carry

        lax.fori_loop(0, count, step, 0)
        copy_x1(u, par).start()

    def tiles(ref, u, at):
        return jnp.concatenate([ref[u, at + g] for g in range(groups)], axis=1)

    def do_x2(u, par):
        copy_x1(u, par).wait_recv()
        if u == 0:
            load_w.wait()
            for sort in range(2):
                weights(sort).wait_recv()
        slot = u % SLOTS
        count = ROWS // 2 // TILE
        half = count // 2
        e_own, e_rx = x1s[u, count * groups].astype(I32), x1r[u, count * groups].astype(I32)
        exponent = (jnp.maximum(e_own, e_rx) + 1).astype(I16)
        x2s[u, 2 * half * groups] = exponent
        inverse = wide(1.0 / scale_of(exponent), groups)
        scale = wide(scale_of(e_rx), groups)
        kept = bit[par] * count

        def both(r):
            f_own = f32_f[slot, rows(kept + r, TILE)]
            f_rx = read_d(tiles(x1r, u, r * groups), scale)
            own = w_own[u // 2, par, rows(kept + r, TILE)].astype(F32)
            other = w_rx[u // 2, par, rows(r, TILE)].astype(F32)
            return f_own + f_rx, f_own * own + f_rx * other

        def send(r, carry):
            denom, numer = both((1 - bit[1 - par]) * half + r)
            d, m = code_d(denom, inverse), code_r(numer, denom)
            for g in range(groups):
                x2s[u, r * groups + g] = d[:, g * LANES:(g + 1) * LANES]
                x2s[u, (half + r) * groups + g] = m[:, g * LANES:(g + 1) * LANES]
            return carry

        lax.fori_loop(0, half, send, 0)
        copy_x2(u, par).start()

        def keep(r, carry):
            denom, numer = both(bit[1 - par] * half + r)
            sums[slot, 0, rows(r, TILE)] = denom
            sums[slot, 1, rows(r, TILE)] = numer
            return carry

        lax.fori_loop(0, half, keep, 0)

    def put(ref, at, code):
        for g in range(groups):
            ref[at + g] = code[:, g * LANES:(g + 1) * LANES]

    def do_z(u, par):
        copy_x2(u, par).wait_recv()
        slot = u % SLOTS
        half = ROWS // 4 // TILE
        e_own, e_rx = x2s[u, 2 * half * groups].astype(I32), x2r[u, 2 * half * groups].astype(I32)
        exponent = (jnp.maximum(e_own, e_rx) + 1).astype(I16)
        inverse = wide(1.0 / scale_of(exponent), groups)
        scale = wide(scale_of(e_rx), groups)

        def four(at):
            d_rx = read_d(tiles(x2r, u, at * groups), scale)
            m_rx = read_r(tiles(x2r, u, (half + at) * groups))
            return sums[slot, 0, rows(at, TILE)] + d_rx, sums[slot, 1, rows(at, TILE)] + d_rx * m_rx

        if u in TREE_Z:
            for n in range(2):
                denom, numer = four((1 - z_bit[par]) * 2 + n)
                put(zas.at[u], n * groups, code_d(denom, inverse))
                put(zas.at[u], (2 + n) * groups, code_r(numer, denom))
            zas[u, 4 * groups] = exponent
            copy_za(u, par).start()
            for n in range(2):
                denom, numer = four(z_bit[par] * 2 + n)
                sums2[slot, 0, n * TILE:(n + 1) * TILE] = denom
                sums2[slot, 1, n * TILE:(n + 1) * TILE] = numer
            return
        for j in (2, 1, 3, 0):
            denom, numer = four(group((zh + j) % 4, par))
            if j == 0:
                mine[slot, 0] = denom
                mine[slot, 1] = numer
                continue
            put(zs.at[u, j - 1], 0, code_d(denom, inverse))
            put(zs.at[u, j - 1], groups, code_r(numer, denom))
            zs[u, j - 1, 2 * groups] = exponent
            copy_z(u, j).start()

    def do_zz(u, par):
        if u not in TREE_Z:
            return
        copy_za(u, par).wait_recv()
        slot = u % SLOTS
        e_own, e_rx = zas[u, 4 * groups].astype(I32), zar[u, 4 * groups].astype(I32)
        exponent = (jnp.maximum(e_own, e_rx) + 1).astype(I16)
        inverse = wide(1.0 / scale_of(exponent), groups)
        scale = wide(scale_of(e_rx), groups)

        def eight(at):
            d_rx = read_d(tiles(zar, u, at * groups), scale)
            m_rx = read_r(tiles(zar, u, (2 + at) * groups))
            return sums2[slot, 0, rows(at, TILE)] + d_rx, sums2[slot, 1, rows(at, TILE)] + d_rx * m_rx

        denom, numer = eight(1 - z_bit[1 - par])
        put(zs.at[u, 0], 0, code_d(denom, inverse))
        put(zs.at[u, 0], groups, code_r(numer, denom))
        zs[u, 0, 2 * groups] = exponent
        copy_zb(u, par).start()
        denom, numer = eight(z_bit[1 - par])
        mine[slot, 0] = denom
        mine[slot, 1] = numer

    def do_merge(u, par):
        slot = u % SLOTS
        denom, numer = mine[slot, 0], mine[slot, 1]
        for j in (1,) if u in TREE_Z else (1, 2, 3):
            (copy_zb(u, par) if u in TREE_Z else copy_z(u, j)).wait_recv()
            scale = wide(scale_of(zr[u, j - 1, 2 * groups].astype(I32)), groups)
            d_rx = read_d(jnp.concatenate([zr[u, j - 1, g] for g in range(groups)], axis=1), scale)
            m_rx = read_r(jnp.concatenate([zr[u, j - 1, groups + g] for g in range(groups)], axis=1))
            denom = denom + d_rx
            numer = numer + d_rx * m_rx
        region(u, par, 16)[...] = (numer / (denom + 1e-6)).astype(BF16)
        if u in TREE_B:
            copy_b1(u, par).start()
        else:
            for j in (2, 1, 3):
                copy_az(u, par, j).start()

    def do_b2(u, par):
        if u in TREE_B:
            copy_b1(u, par).wait_recv()
            copy_b2(u, par).start()

    def do_a1(u, par):
        if u in TREE_B:
            copy_b2(u, par).wait_recv()
        else:
            for j in (1, 2, 3):
                copy_az(u, par, j).wait_recv()
        if u in DIRECT_X:
            for copy in copies_ad(u, par):
                copy.start()
        else:
            copy_a1(u, par).start()

    def do_a2(u, par):
        if u not in DIRECT_X:
            copy_a1(u, par).wait_recv()
            copy_a2(u, par).start()

    def do_out(u, par):
        if u in DIRECT_X:
            for copy in copies_ad(u, par):
                copy.wait_recv()
        else:
            copy_a2(u, par).wait_recv()
        copy_out(u).start()

    load_acts.wait()
    pl.semaphore_wait(barrier, len(others))
    for par in range(2):
        weights(par).start()

    stages = (do_turn, do_y1, do_y2, do_core, do_fisher, do_x2, do_z, do_zz, do_merge,
              do_b2, do_a1, do_a2, do_out)
    for step in ORDER:
        stages[step // UNITS](step % UNITS, step % UNITS % 2)

    for par in range(2):
        weights(par).wait_send()

    for u in range(UNITS):
        par = u % 2
        sent = [copy_zl(u, par), copy_y0(u, par), copy_y2(u, par), copy_core(u, par),
                copy_x1(u, par), copy_x2(u, par)]
        if u not in LATE_ZL:
            sent.append(copy_y1(u, par))
        sent += [copy_za(u, par), copy_zb(u, par)] if u in TREE_Z else [copy_z(u, j) for j in (1, 2, 3)]
        sent += [copy_b1(u, par), copy_b2(u, par)] if u in TREE_B else [copy_az(u, par, j) for j in (1, 2, 3)]
        sent += copies_ad(u, par) if u in DIRECT_X else [copy_a1(u, par), copy_a2(u, par)]
        for copy in sent:
            copy.wait_send()
        copy_out(u).wait()


def body(acts, cotangent, seq_lengths, up_weight):
    tokens, cols = cotangent.shape[1:]
    width = acts.shape[2]
    groups = cols // LANES
    any_space = pl.BlockSpec(memory_space=pl.ANY)
    half, quarter = ROWS // 2 // TILE, ROWS // 4 // TILE
    merged = pl.pallas_call(
        kernel,
        out_shape=jax.ShapeDtypeStruct((UNITS, ROWS, cols), BF16),
        in_specs=[pl.BlockSpec(memory_space=pltpu.SMEM), any_space, any_space, any_space],
        out_specs=any_space,
        scratch_shapes=[
            pltpu.VMEM((acts.shape[1], width), BF16),
            pltpu.VMEM((2, 2, 2, 2, UNITS, ROWS, LANES), BF16),
            pltpu.VMEM((tokens, cols), BF16),
            pltpu.VMEM((UNITS // 2, 2, ROWS, cols), BF16),
            pltpu.VMEM((UNITS // 2, 2, ROWS // 2, cols), BF16),
            pltpu.VMEM((SLOTS, ROWS, cols), F32),
            pltpu.VMEM((SLOTS, 2, ROWS // 4, cols), F32),
            pltpu.VMEM((SLOTS, 2, 2 * TILE, cols), F32),
            pltpu.VMEM((SLOTS, 2, TILE, cols), F32),
            pltpu.VMEM((UNITS, half * groups + 1, TILE, LANES), I16),
            pltpu.VMEM((UNITS, half * groups + 1, TILE, LANES), I16),
            pltpu.VMEM((UNITS, 2 * quarter * groups + 1, TILE, LANES), I16),
            pltpu.VMEM((UNITS, 2 * quarter * groups + 1, TILE, LANES), I16),
            pltpu.VMEM((UNITS, 4 * groups + 1, TILE, LANES), I16),
            pltpu.VMEM((UNITS, 4 * groups + 1, TILE, LANES), I16),
            pltpu.VMEM((UNITS, 3, 2 * groups + 1, TILE, LANES), I16),
            pltpu.VMEM((UNITS, 3, 2 * groups + 1, TILE, LANES), I16),
            pltpu.VMEM((UNITS, ROWS, cols), BF16),
            pltpu.SemaphoreType.DMA((3,)),
            pltpu.SemaphoreType.DMA((2,)),
            pltpu.SemaphoreType.DMA((2,)),
            pltpu.SemaphoreType.DMA((12, UNITS)),
            pltpu.SemaphoreType.DMA((12, UNITS)),
            pltpu.SemaphoreType.DMA((UNITS, 3)),
            pltpu.SemaphoreType.DMA((UNITS, 3)),
            pltpu.SemaphoreType.DMA((UNITS, 3)),
            pltpu.SemaphoreType.DMA((UNITS, 3)),
            pltpu.SemaphoreType.DMA((UNITS, 3)),
            pltpu.SemaphoreType.DMA((UNITS, 3)),
            pltpu.SemaphoreType.DMA((UNITS,)),
        ],
        compiler_params=pltpu.CompilerParams(
            collective_id=0, has_side_effects=True, vmem_limit_bytes=58 * 2**20),
    )(seq_lengths, acts[0], cotangent[0], up_weight[0].reshape(UNITS // 2, 2, ROWS, cols))
    return merged.reshape(width, cols)


def solution(mesh):
    in_specs = (
        P("ckpt", "tensor", None),
        P("ckpt", None, "tensor"),
        P(),
        P("ckpt", None, "tensor"),
    )
    out_specs = P(None, "tensor")
    return jax.shard_map(body, mesh=mesh, in_specs=in_specs, out_specs=out_specs, check_vma=False)
```

```python
import jax
import jax.numpy as jnp
from jax import lax
from jax.experimental import pallas as pl
from jax.experimental.pallas import tpu as pltpu
from jax.sharding import PartitionSpec as P

MESH = pl.DeviceIdType.MESH
LATE_ZL = (0,)
TREE_Z = (0, 1, 2, 3, 4, 5, 6, 7, 8, 9)
TREE_B = ()
DIRECT_X = (12, 13)
ORDER = (
    0, 1, 2, 3, 4, 5, 14, 6, 15, 16, 17, 18, 28, 7, 8, 19,
    29, 30, 31, 42, 32, 20, 43, 21, 56, 57, 9, 33, 22, 44, 58, 70,
    45, 23, 71, 46, 34, 35, 10, 59, 11, 60, 72, 84, 47, 24, 36, 85,
    73, 37, 12, 61, 25, 13, 48, 86, 98, 74, 62, 49, 87, 75, 99, 63,
    112, 100, 126, 50, 88, 38, 76, 113, 64, 39, 89, 51, 140, 127, 101, 77,
    114, 128, 26, 65, 102, 90, 78, 154, 27, 52, 115, 91, 66, 103, 53, 79,
    40, 41, 129, 141, 142, 168, 104, 116, 67, 92, 117, 80, 143, 118, 93, 81,
    130, 144, 105, 54, 106, 155, 131, 156, 94, 157, 55, 132, 68, 107, 69, 119,
    145, 169, 95, 158, 120, 170, 133, 108, 134, 171, 121, 109, 135, 146, 82, 147,
    83, 159, 160, 122, 172, 123, 136, 96, 148, 161, 149, 173, 97, 150, 137, 151,
    110, 162, 174, 111, 163, 175, 124, 138, 164, 165, 125, 176, 139, 177, 152, 178,
    179, 166, 153, 167, 180, 181,
)
F32, BF16, I16, I32 = jnp.float32, jnp.bfloat16, jnp.int16, jnp.int32
UNITS = 14
ROWS = 256
LANES = 128
TILE = 16
SLOTS = 14
D_TOP = 65504.0
D_MID = 32752
R_TOP = 32704.0
W_MAX = 0.125


def fourth_root(v):
    return jnp.sqrt(jnp.sqrt(v))


def wide(tile, count):
    return jnp.concatenate([tile] * count, axis=1)


def scale_of(exponent):
    return jnp.exp2(exponent.astype(F32))


def code_d(v, inverse):
    root = fourth_root(v * inverse)
    code = (root * D_TOP + 0.5).astype(I32) - D_MID
    return jnp.minimum(code, 32767).astype(I16)


def read_d(code, scale):
    root = (code.astype(F32) + float(D_MID)) * (1.0 / D_TOP)
    square = root * root
    return square * square * scale


def code_r(numer, denom):
    mean = numer / jnp.maximum(denom, 1e-30)
    root = fourth_root(jnp.minimum(jnp.abs(mean) * (1.0 / W_MAX), 1.0))
    code = (root * R_TOP + 0.5).astype(I32)
    return jnp.where(mean < 0.0, -code, code).astype(I16)


def read_r(code):
    value = code.astype(F32)
    root = value * (1.0 / R_TOP)
    square = root * root
    return square * square * jnp.where(value < 0.0, -W_MAX, W_MAX)


def kernel(seq_ref, acts_hbm, cot_hbm, w_hbm, out,
           acts, xt, cot, w_own, w_rx, f32_f, sums, sums2, mine,
           x1s, x1r, x2s, x2r, zas, zar, zs, zr,
           load_sem, s_w, r_w, s_one, r_one, s_z, r_z, s_az, r_az, s_ad, r_ad):
    cols = cot.shape[1]
    groups = cols // LANES
    seq_count = seq_ref.shape[0]
    seq_len = cot.shape[0] // seq_count
    ck, tn = lax.axis_index("ckpt"), lax.axis_index("tensor")
    x, zh = ck // 4, ck % 4
    zl, y, core = tn // 8, (tn // 2) % 4, tn % 2
    xa, xb = ((x + 1) // 2) % 2, x // 2
    ya, yb = ((y + 1) // 2) % 2, y // 2
    to_zl = (ck, (1 - zl) * 8 + y * 2 + core)
    to_core = (ck, zl * 8 + y * 2 + 1 - core)
    to_y = [(ck, zl * 8 + (y + 1 - 2 * (y % 2)) * 2 + core), (ck, zl * 8 + (3 - y) * 2 + core)]
    to_x = [((x + 1 - 2 * (x % 2)) * 4 + zh, tn), ((3 - x) * 4 + zh, tn)]
    to_far_x = ((x + 2) % 4 * 4 + zh, tn)
    to_z = [(x * 4 + (zh + j) % 4, tn) for j in range(4)]
    to_zp = [(x * 4 + zh + 1 - 2 * (zh % 2), tn), (x * 4 + 3 - zh, tn)]
    bit = [xa, xb]

    def z_bits(n):
        return [((n + 1) // 2) % 2, n // 2]

    def group(n, par):
        bits = z_bits(n)
        return bits[par] * 2 + bits[1 - par]

    z_bit = z_bits(zh)
    ZL, Y0, Y1, Y2, CO, X1, X2, ZA, B1, B2, A1, A2 = range(12)

    barrier = pltpu.get_barrier_semaphore()
    others = [to_zl, to_core, *to_y, *to_x, to_far_x, *to_z[1:]]
    for other in others:
        pl.semaphore_signal(barrier, 1, device_id=other, device_id_type=MESH)

    load_acts = pltpu.make_async_copy(acts_hbm, acts, load_sem.at[0])
    load_cot = pltpu.make_async_copy(cot_hbm, cot, load_sem.at[1])
    load_w = pltpu.make_async_copy(w_hbm, w_own, load_sem.at[2])
    load_acts.start()
    load_cot.start()
    load_w.start()

    def rows(n, size):
        return pl.ds(pl.multiple_of(n * size, size), size)

    def remote(src, dst, send, recv, to):
        return pltpu.make_async_remote_copy(src, dst, send, recv, device_id=to, device_id_type=MESH)

    def one(stage, u, ref, to):
        return remote(ref, ref, s_one.at[stage, u], r_one.at[stage, u], to)

    def weights(par):
        return remote(w_hbm.at[:, par, rows(1 - bit[par], ROWS // 2)], w_rx.at[:, par],
                      s_w.at[par], r_w.at[par], to_x[par])

    def copy_zl(u, par):
        ref = xt.at[zl, :, :, core, u] if u in LATE_ZL else xt.at[zl, yb, ya, core, u]
        return one(ZL, u, ref, to_zl)

    def copy_y0(u, par):
        return one(Y0, u, xt.at[zl, yb, ya, core, u], to_y[par])

    def copy_y1(u, par):
        return one(Y1, u, xt.at[1 - zl, yb, ya, core, u], to_y[par])

    def copy_y2(u, par):
        layer = zl if u in LATE_ZL else slice(None)
        ref = xt.at[layer, yb, :, core, u] if par == 0 else xt.at[layer, :, ya, core, u]
        return one(Y2, u, ref, to_y[1 - par])

    def copy_core(u, par):
        return one(CO, u, xt.at[:, :, :, core, u], to_core)

    def copy_x1(u, par):
        return remote(x1s.at[u], x1r.at[u], s_one.at[X1, u], r_one.at[X1, u], to_x[par])

    def copy_x2(u, par):
        return remote(x2s.at[u], x2r.at[u], s_one.at[X2, u], r_one.at[X2, u], to_x[1 - par])

    def copy_z(u, j):
        return remote(zs.at[u, j - 1], zr.at[u, j - 1], s_z.at[u, j - 1], r_z.at[u, j - 1], to_z[j])

    def region(u, par, size):
        first, second = bit[par], bit[1 - par]
        if size == 128:
            return out.at[u, rows(first, 128)]
        if size == 64:
            return out.at[u, rows(first * 2 + second, 64)]
        if size == 32:
            return out.at[u, rows(first * 4 + second * 2 + z_bit[par], 32)]
        return out.at[u, rows(first * 8 + second * 4 + group(zh, par), 16)]

    def copy_za(u, par):
        return remote(zas.at[u], zar.at[u], s_one.at[ZA, u], r_one.at[ZA, u], to_zp[par])

    def copy_zb(u, par):
        return remote(zs.at[u, 0], zr.at[u, 0], s_z.at[u, 0], r_z.at[u, 0], to_zp[1 - par])

    def copy_b1(u, par):
        return one(B1, u, region(u, par, 16), to_zp[1 - par])

    def copy_b2(u, par):
        return one(B2, u, region(u, par, 32), to_zp[par])

    def copies_ad(u, par):
        ref = region(u, par, 64)
        return [remote(ref, ref, s_ad.at[u, k], r_ad.at[u, k], to)
                for k, to in enumerate((*to_x, to_far_x))]

    def copy_az(u, par, j):
        ref = region(u, par, 16)
        return remote(ref, ref, s_az.at[u, j - 1], r_az.at[u, j - 1], to_z[j])

    def copy_a1(u, par):
        return one(A1, u, region(u, par, 64), to_x[1 - par])

    def copy_a2(u, par):
        return one(A2, u, region(u, par, 128), to_x[par])

    def turn(u):
        block = acts[:, pl.ds(pl.multiple_of(u * ROWS, ROWS), ROWS)]
        xt[zl, yb, ya, core, u] = block.astype(F32).T.astype(BF16)

    def mask(b, carry):
        size = 64
        seq = b // (seq_len // size)
        at = (b % (seq_len // size)) * size
        block = cot[rows(b, size)].astype(F32)
        position = lax.broadcasted_iota(I32, (size, cols), 0) + at
        cot[rows(b, size)] = jnp.where(position < seq_ref[seq], block, 0.0).astype(BF16)
        return carry

    def do_turn(u, par):
        turn(u)
        if u not in LATE_ZL:
            copy_zl(u, par).start()
        copy_y0(u, par).start()

    def do_y1(u, par):
        if u in LATE_ZL:
            copy_y0(u, par).wait_recv()
            copy_y2(u, par).start()
        else:
            copy_zl(u, par).wait_recv()
            copy_y1(u, par).start()

    def do_y2(u, par):
        if u in LATE_ZL:
            copy_y2(u, par).wait_recv()
            copy_zl(u, par).start()
        else:
            copy_y0(u, par).wait_recv()
            copy_y1(u, par).wait_recv()
            copy_y2(u, par).start()

    def do_core(u, par):
        (copy_zl if u in LATE_ZL else copy_y2)(u, par).wait_recv()
        copy_core(u, par).start()

    def do_fisher(u, par):
        copy_core(u, par).wait_recv()
        if u == 0:
            load_cot.wait()
            lax.fori_loop(0, cot.shape[0] // 64, mask, 0)
        slot = u % SLOTS
        total = None
        for seq in range(seq_count):
            near, far = seq // 2, seq % 2
            order = (0, 1) if far == 0 else (1, 0)
            left = jnp.concatenate(
                [xt[near, far, a, c, u] for a in order for c in range(2)], axis=1)
            grad = jnp.dot(left, cot[seq * seq_len:(seq + 1) * seq_len, :], preferred_element_type=F32)
            total = grad * grad if total is None else total + grad * grad
        f32_f[slot] = total
        most = total[:, :LANES]
        for g in range(1, groups):
            most = jnp.maximum(most, total[:, g * LANES:(g + 1) * LANES])
        top = most[:TILE]
        for r in range(1, ROWS // TILE):
            top = jnp.maximum(top, most[r * TILE:(r + 1) * TILE])
        exponent = jnp.ceil(jnp.log2(jnp.maximum(top, 1e-30)) + 0.01).astype(I32).astype(I16)
        count = ROWS // 2 // TILE
        x1s[u, count * groups] = exponent
        inverse = wide(1.0 / scale_of(exponent), groups)
        base = (1 - bit[par]) * count

        def step(r, carry):
            code = code_d(f32_f[slot, rows(base + r, TILE)], inverse)
            for g in range(groups):
                x1s[u, r * groups + g] = code[:, g * LANES:(g + 1) * LANES]
            return carry

        lax.fori_loop(0, count, step, 0)
        copy_x1(u, par).start()

    def tiles(ref, u, at):
        return jnp.concatenate([ref[u, at + g] for g in range(groups)], axis=1)

    def do_x2(u, par):
        copy_x1(u, par).wait_recv()
        if u == 0:
            load_w.wait()
            for sort in range(2):
                weights(sort).wait_recv()
        slot = u % SLOTS
        count = ROWS // 2 // TILE
        half = count // 2
        e_own, e_rx = x1s[u, count * groups].astype(I32), x1r[u, count * groups].astype(I32)
        exponent = (jnp.maximum(e_own, e_rx) + 1).astype(I16)
        x2s[u, 2 * half * groups] = exponent
        inverse = wide(1.0 / scale_of(exponent), groups)
        scale = wide(scale_of(e_rx), groups)
        kept = bit[par] * count

        def both(r):
            f_own = f32_f[slot, rows(kept + r, TILE)]
            f_rx = read_d(tiles(x1r, u, r * groups), scale)
            own = w_own[u // 2, par, rows(kept + r, TILE)].astype(F32)
            other = w_rx[u // 2, par, rows(r, TILE)].astype(F32)
            return f_own + f_rx, f_own * own + f_rx * other

        def send(r, carry):
            denom, numer = both((1 - bit[1 - par]) * half + r)
            d, m = code_d(denom, inverse), code_r(numer, denom)
            for g in range(groups):
                x2s[u, r * groups + g] = d[:, g * LANES:(g + 1) * LANES]
                x2s[u, (half + r) * groups + g] = m[:, g * LANES:(g + 1) * LANES]
            return carry

        lax.fori_loop(0, half, send, 0)
        copy_x2(u, par).start()

        def keep(r, carry):
            denom, numer = both(bit[1 - par] * half + r)
            sums[slot, 0, rows(r, TILE)] = denom
            sums[slot, 1, rows(r, TILE)] = numer
            return carry

        lax.fori_loop(0, half, keep, 0)

    def put(ref, at, code):
        for g in range(groups):
            ref[at + g] = code[:, g * LANES:(g + 1) * LANES]

    def do_z(u, par):
        copy_x2(u, par).wait_recv()
        slot = u % SLOTS
        half = ROWS // 4 // TILE
        e_own, e_rx = x2s[u, 2 * half * groups].astype(I32), x2r[u, 2 * half * groups].astype(I32)
        exponent = (jnp.maximum(e_own, e_rx) + 1).astype(I16)
        inverse = wide(1.0 / scale_of(exponent), groups)
        scale = wide(scale_of(e_rx), groups)

        def four(at):
            d_rx = read_d(tiles(x2r, u, at * groups), scale)
            m_rx = read_r(tiles(x2r, u, (half + at) * groups))
            return sums[slot, 0, rows(at, TILE)] + d_rx, sums[slot, 1, rows(at, TILE)] + d_rx * m_rx

        if u in TREE_Z:
            for n in range(2):
                denom, numer = four((1 - z_bit[par]) * 2 + n)
                put(zas.at[u], n * groups, code_d(denom, inverse))
                put(zas.at[u], (2 + n) * groups, code_r(numer, denom))
            zas[u, 4 * groups] = exponent
            copy_za(u, par).start()
            for n in range(2):
                denom, numer = four(z_bit[par] * 2 + n)
                sums2[slot, 0, n * TILE:(n + 1) * TILE] = denom
                sums2[slot, 1, n * TILE:(n + 1) * TILE] = numer
            return
        for j in (2, 1, 3, 0):
            denom, numer = four(group((zh + j) % 4, par))
            if j == 0:
                mine[slot, 0] = denom
                mine[slot, 1] = numer
                continue
            put(zs.at[u, j - 1], 0, code_d(denom, inverse))
            put(zs.at[u, j - 1], groups, code_r(numer, denom))
            zs[u, j - 1, 2 * groups] = exponent
            copy_z(u, j).start()

    def do_zz(u, par):
        if u not in TREE_Z:
            return
        copy_za(u, par).wait_recv()
        slot = u % SLOTS
        e_own, e_rx = zas[u, 4 * groups].astype(I32), zar[u, 4 * groups].astype(I32)
        exponent = (jnp.maximum(e_own, e_rx) + 1).astype(I16)
        inverse = wide(1.0 / scale_of(exponent), groups)
        scale = wide(scale_of(e_rx), groups)

        def eight(at):
            d_rx = read_d(tiles(zar, u, at * groups), scale)
            m_rx = read_r(tiles(zar, u, (2 + at) * groups))
            return sums2[slot, 0, rows(at, TILE)] + d_rx, sums2[slot, 1, rows(at, TILE)] + d_rx * m_rx

        denom, numer = eight(1 - z_bit[1 - par])
        put(zs.at[u, 0], 0, code_d(denom, inverse))
        put(zs.at[u, 0], groups, code_r(numer, denom))
        zs[u, 0, 2 * groups] = exponent
        copy_zb(u, par).start()
        denom, numer = eight(z_bit[1 - par])
        mine[slot, 0] = denom
        mine[slot, 1] = numer

    def do_merge(u, par):
        slot = u % SLOTS
        denom, numer = mine[slot, 0], mine[slot, 1]
        for j in (1,) if u in TREE_Z else (1, 2, 3):
            (copy_zb(u, par) if u in TREE_Z else copy_z(u, j)).wait_recv()
            scale = wide(scale_of(zr[u, j - 1, 2 * groups].astype(I32)), groups)
            d_rx = read_d(jnp.concatenate([zr[u, j - 1, g] for g in range(groups)], axis=1), scale)
            m_rx = read_r(jnp.concatenate([zr[u, j - 1, groups + g] for g in range(groups)], axis=1))
            denom = denom + d_rx
            numer = numer + d_rx * m_rx
        region(u, par, 16)[...] = (numer / (denom + 1e-6)).astype(BF16)
        if u in TREE_B:
            copy_b1(u, par).start()
        else:
            for j in (2, 1, 3):
                copy_az(u, par, j).start()

    def do_b2(u, par):
        if u in TREE_B:
            copy_b1(u, par).wait_recv()
            copy_b2(u, par).start()

    def do_a1(u, par):
        if u in TREE_B:
            copy_b2(u, par).wait_recv()
        else:
            for j in (1, 2, 3):
                copy_az(u, par, j).wait_recv()
        if u in DIRECT_X:
            for copy in copies_ad(u, par):
                copy.start()
        else:
            copy_a1(u, par).start()

    def do_a2(u, par):
        if u not in DIRECT_X:
            copy_a1(u, par).wait_recv()
            copy_a2(u, par).start()

    def do_out(u, par):
        if u in DIRECT_X:
            for copy in copies_ad(u, par):
                copy.wait_recv()
        else:
            copy_a2(u, par).wait_recv()

    load_acts.wait()
    pl.semaphore_wait(barrier, len(others))
    for par in range(2):
        weights(par).start()

    stages = (do_turn, do_y1, do_y2, do_core, do_fisher, do_x2, do_z, do_zz, do_merge,
              do_b2, do_a1, do_a2, do_out)
    for step in ORDER:
        stages[step // UNITS](step % UNITS, step % UNITS % 2)

    for par in range(2):
        weights(par).wait_send()

    for u in range(UNITS):
        par = u % 2
        sent = [copy_zl(u, par), copy_y0(u, par), copy_y2(u, par), copy_core(u, par),
                copy_x1(u, par), copy_x2(u, par)]
        if u not in LATE_ZL:
            sent.append(copy_y1(u, par))
        sent += [copy_za(u, par), copy_zb(u, par)] if u in TREE_Z else [copy_z(u, j) for j in (1, 2, 3)]
        sent += [copy_b1(u, par), copy_b2(u, par)] if u in TREE_B else [copy_az(u, par, j) for j in (1, 2, 3)]
        sent += copies_ad(u, par) if u in DIRECT_X else [copy_a1(u, par), copy_a2(u, par)]
        for copy in sent:
            copy.wait_send()


def body(acts, cotangent, seq_lengths, up_weight):
    tokens, cols = cotangent.shape[1:]
    width = acts.shape[2]
    groups = cols // LANES
    any_space = pl.BlockSpec(memory_space=pl.ANY)
    half, quarter = ROWS // 2 // TILE, ROWS // 4 // TILE
    merged = pl.pallas_call(
        kernel,
        out_shape=pltpu.VMEM((UNITS, ROWS, cols), BF16),
        in_specs=[pl.BlockSpec(memory_space=pltpu.SMEM), any_space, any_space, any_space],
        out_specs=pl.BlockSpec(memory_space=pltpu.VMEM),
        scratch_shapes=[
            pltpu.VMEM((acts.shape[1], width), BF16),
            pltpu.VMEM((2, 2, 2, 2, UNITS, ROWS, LANES), BF16),
            pltpu.VMEM((tokens, cols), BF16),
            pltpu.VMEM((UNITS // 2, 2, ROWS, cols), BF16),
            pltpu.VMEM((UNITS // 2, 2, ROWS // 2, cols), BF16),
            pltpu.VMEM((SLOTS, ROWS, cols), F32),
            pltpu.VMEM((SLOTS, 2, ROWS // 4, cols), F32),
            pltpu.VMEM((SLOTS, 2, 2 * TILE, cols), F32),
            pltpu.VMEM((SLOTS, 2, TILE, cols), F32),
            pltpu.VMEM((UNITS, half * groups + 1, TILE, LANES), I16),
            pltpu.VMEM((UNITS, half * groups + 1, TILE, LANES), I16),
            pltpu.VMEM((UNITS, 2 * quarter * groups + 1, TILE, LANES), I16),
            pltpu.VMEM((UNITS, 2 * quarter * groups + 1, TILE, LANES), I16),
            pltpu.VMEM((UNITS, 4 * groups + 1, TILE, LANES), I16),
            pltpu.VMEM((UNITS, 4 * groups + 1, TILE, LANES), I16),
            pltpu.VMEM((UNITS, 3, 2 * groups + 1, TILE, LANES), I16),
            pltpu.VMEM((UNITS, 3, 2 * groups + 1, TILE, LANES), I16),
            pltpu.SemaphoreType.DMA((3,)),
            pltpu.SemaphoreType.DMA((2,)),
            pltpu.SemaphoreType.DMA((2,)),
            pltpu.SemaphoreType.DMA((12, UNITS)),
            pltpu.SemaphoreType.DMA((12, UNITS)),
            pltpu.SemaphoreType.DMA((UNITS, 3)),
            pltpu.SemaphoreType.DMA((UNITS, 3)),
            pltpu.SemaphoreType.DMA((UNITS, 3)),
            pltpu.SemaphoreType.DMA((UNITS, 3)),
            pltpu.SemaphoreType.DMA((UNITS, 3)),
            pltpu.SemaphoreType.DMA((UNITS, 3)),
        ],
        compiler_params=pltpu.CompilerParams(
            collective_id=0, has_side_effects=True, vmem_limit_bytes=54 * 2**20),
    )(seq_lengths, acts[0], cotangent[0], up_weight[0].reshape(UNITS // 2, 2, ROWS, cols))
    return merged.reshape(width, cols)


def solution(mesh):
    in_specs = (
        P("ckpt", "tensor", None),
        P("ckpt", None, "tensor"),
        P(),
        P("ckpt", None, "tensor"),
    )
    out_specs = P(None, "tensor")
    return jax.shard_map(body, mesh=mesh, in_specs=in_specs, out_specs=out_specs, check_vma=False)
```

```python
import jax
import jax.numpy as jnp
from jax import lax
from jax.experimental import pallas as pl
from jax.experimental.pallas import tpu as pltpu
from jax.sharding import PartitionSpec as P

MESH = pl.DeviceIdType.MESH
LATE_ZL = (0, 3)
TREE_Z = (0, 1, 2, 3, 4, 5, 6, 7, 8, 9, 10, 11)
TREE_B = ()
DIRECT_X = (12, 13)
TURNED = 4
ORDER = (
    0, 1, 2, 3, 4, 5, 14, 6, 15, 16, 17, 7, 18, 19, 28, 29,
    20, 21, 8, 30, 31, 42, 9, 22, 43, 32, 56, 33, 34, 57, 44, 58,
    45, 35, 10, 70, 71, 23, 46, 36, 59, 60, 11, 47, 24, 72, 84, 85,
    48, 61, 73, 25, 37, 12, 62, 86, 74, 49, 38, 98, 26, 99, 87, 63,
    50, 75, 13, 112, 76, 64, 39, 51, 113, 100, 27, 88, 77, 65, 126, 89,
    101, 52, 90, 140, 78, 127, 40, 141, 114, 66, 53, 41, 102, 91, 79, 67,
    128, 115, 129, 103, 154, 80, 155, 54, 104, 116, 92, 130, 142, 81, 55, 93,
    143, 117, 168, 68, 94, 144, 69, 105, 95, 169, 156, 106, 107, 131, 157, 158,
    82, 118, 108, 119, 132, 109, 145, 83, 170, 120, 171, 146, 133, 121, 134, 135,
    172, 159, 122, 147, 160, 123, 136, 96, 148, 137, 149, 161, 173, 150, 97, 151,
    110, 174, 162, 163, 124, 111, 175, 164, 165, 125, 176, 138, 152, 177, 166, 178,
    179, 139, 153, 180, 167, 181,
)
F32, BF16, I16, I32 = jnp.float32, jnp.bfloat16, jnp.int16, jnp.int32
UNITS = 14
ROWS = 256
LANES = 128
TILE = 16
SLOTS = 14
D_TOP = 65504.0
D_MID = 32752
R_TOP = 32704.0
W_MAX = 0.125


def fourth_root(v):
    return jnp.sqrt(jnp.sqrt(v))


def wide(tile, count):
    return jnp.concatenate([tile] * count, axis=1)


def scale_of(exponent):
    return jnp.exp2(exponent.astype(F32))


def code_d(v, inverse):
    root = fourth_root(v * inverse)
    code = (root * D_TOP + 0.5).astype(I32) - D_MID
    return jnp.minimum(code, 32767).astype(I16)


def read_d(code, scale):
    root = (code.astype(F32) + float(D_MID)) * (1.0 / D_TOP)
    square = root * root
    return square * square * scale


def code_r(numer, denom):
    mean = numer / jnp.maximum(denom, 1e-30)
    root = fourth_root(jnp.minimum(jnp.abs(mean) * (1.0 / W_MAX), 1.0))
    code = (root * R_TOP + 0.5).astype(I32)
    return jnp.where(mean < 0.0, -code, code).astype(I16)


def read_r(code):
    value = code.astype(F32)
    root = value * (1.0 / R_TOP)
    square = root * root
    return square * square * jnp.where(value < 0.0, -W_MAX, W_MAX)


def kernel(seq_ref, acts_hbm, cot_hbm, w_hbm, out,
           acts, xt, cot, w_own, w_rx, f32_f, sums, sums2, mine,
           x1s, x1r, x2s, x2r, zas, zar, zs, zr,
           load_sem, s_w, r_w, s_one, r_one, s_z, r_z, s_az, r_az, s_ad, r_ad):
    cols = cot.shape[1]
    groups = cols // LANES
    seq_count = seq_ref.shape[0]
    seq_len = cot.shape[0] // seq_count
    ck, tn = lax.axis_index("ckpt"), lax.axis_index("tensor")
    x, zh = ck // 4, ck % 4
    zl, y, core = tn // 8, (tn // 2) % 4, tn % 2
    xa, xb = ((x + 1) // 2) % 2, x // 2
    ya, yb = ((y + 1) // 2) % 2, y // 2
    to_zl = (ck, (1 - zl) * 8 + y * 2 + core)
    to_core = (ck, zl * 8 + y * 2 + 1 - core)
    to_y = [(ck, zl * 8 + (y + 1 - 2 * (y % 2)) * 2 + core), (ck, zl * 8 + (3 - y) * 2 + core)]
    to_x = [((x + 1 - 2 * (x % 2)) * 4 + zh, tn), ((3 - x) * 4 + zh, tn)]
    to_far_x = ((x + 2) % 4 * 4 + zh, tn)
    to_z = [(x * 4 + (zh + j) % 4, tn) for j in range(4)]
    to_zp = [(x * 4 + zh + 1 - 2 * (zh % 2), tn), (x * 4 + 3 - zh, tn)]
    bit = [xa, xb]

    def z_bits(n):
        return [((n + 1) // 2) % 2, n // 2]

    def group(n, par):
        bits = z_bits(n)
        return bits[par] * 2 + bits[1 - par]

    z_bit = z_bits(zh)
    ZL, Y0, Y1, Y2, CO, X1, X2, ZA, B1, B2, A1, A2 = range(12)

    barrier = pltpu.get_barrier_semaphore()
    others = [to_zl, to_core, *to_y, *to_x, to_far_x, *to_z[1:]]
    for other in others:
        pl.semaphore_signal(barrier, 1, device_id=other, device_id_type=MESH)

    load_acts = pltpu.make_async_copy(acts_hbm, acts, load_sem.at[0])
    load_cot = pltpu.make_async_copy(cot_hbm, cot, load_sem.at[1])
    load_w = pltpu.make_async_copy(w_hbm, w_own, load_sem.at[2])
    load_acts.start()
    load_cot.start()
    load_w.start()

    def rows(n, size):
        return pl.ds(pl.multiple_of(n * size, size), size)

    def remote(src, dst, send, recv, to):
        return pltpu.make_async_remote_copy(src, dst, send, recv, device_id=to, device_id_type=MESH)

    def one(stage, u, ref, to):
        return remote(ref, ref, s_one.at[stage, u], r_one.at[stage, u], to)

    def weights(par):
        return remote(w_hbm.at[:, par, rows(1 - bit[par], ROWS // 2)], w_rx.at[:, par],
                      s_w.at[par], r_w.at[par], to_x[par])

    def copy_zl(u, par):
        ref = xt.at[zl, :, :, core, u] if u in LATE_ZL else xt.at[zl, yb, ya, core, u]
        return one(ZL, u, ref, to_zl)

    def copy_y0(u, par):
        return one(Y0, u, xt.at[zl, yb, ya, core, u], to_y[par])

    def copy_y1(u, par):
        return one(Y1, u, xt.at[1 - zl, yb, ya, core, u], to_y[par])

    def copy_y2(u, par):
        layer = zl if u in LATE_ZL else slice(None)
        ref = xt.at[layer, yb, :, core, u] if par == 0 else xt.at[layer, :, ya, core, u]
        return one(Y2, u, ref, to_y[1 - par])

    def copy_core(u, par):
        return one(CO, u, xt.at[:, :, :, core, u], to_core)

    def copy_x1(u, par):
        return remote(x1s.at[u], x1r.at[u], s_one.at[X1, u], r_one.at[X1, u], to_x[par])

    def copy_x2(u, par):
        return remote(x2s.at[u], x2r.at[u], s_one.at[X2, u], r_one.at[X2, u], to_x[1 - par])

    def copy_z(u, j):
        return remote(zs.at[u, j - 1], zr.at[u, j - 1], s_z.at[u, j - 1], r_z.at[u, j - 1], to_z[j])

    def region(u, par, size):
        first, second = bit[par], bit[1 - par]
        if size == 128:
            return out.at[u, rows(first, 128)]
        if size == 64:
            return out.at[u, rows(first * 2 + second, 64)]
        if size == 32:
            return out.at[u, rows(first * 4 + second * 2 + z_bit[par], 32)]
        return out.at[u, rows(first * 8 + second * 4 + group(zh, par), 16)]

    def copy_za(u, par):
        return remote(zas.at[u], zar.at[u], s_one.at[ZA, u], r_one.at[ZA, u], to_zp[par])

    def copy_zb(u, par):
        return remote(zs.at[u, 0], zr.at[u, 0], s_z.at[u, 0], r_z.at[u, 0], to_zp[1 - par])

    def copy_b1(u, par):
        return one(B1, u, region(u, par, 16), to_zp[1 - par])

    def copy_b2(u, par):
        return one(B2, u, region(u, par, 32), to_zp[par])

    def copies_ad(u, par):
        ref = region(u, par, 64)
        return [remote(ref, ref, s_ad.at[u, k], r_ad.at[u, k], to)
                for k, to in enumerate((*to_x, to_far_x))]

    def copy_az(u, par, j):
        ref = region(u, par, 16)
        return remote(ref, ref, s_az.at[u, j - 1], r_az.at[u, j - 1], to_z[j])

    def copy_a1(u, par):
        return one(A1, u, region(u, par, 64), to_x[1 - par])

    def copy_a2(u, par):
        return one(A2, u, region(u, par, 128), to_x[par])

    def turn(u):
        block = acts[:, pl.ds(pl.multiple_of(u * ROWS, ROWS), ROWS)]
        xt[zl, yb, ya, core, u] = block.astype(F32).T.astype(BF16)

    def mask(b, carry):
        size = 64
        seq = b // (seq_len // size)
        at = (b % (seq_len // size)) * size
        block = cot[rows(b, size)].astype(F32)
        position = lax.broadcasted_iota(I32, (size, cols), 0) + at
        cot[rows(b, size)] = jnp.where(position < seq_ref[seq], block, 0.0).astype(BF16)
        return carry

    def do_turn(u, par):
        if u >= TURNED:
            turn(u)
        if u not in LATE_ZL:
            copy_zl(u, par).start()
        copy_y0(u, par).start()

    def do_y1(u, par):
        if u == 0:
            load_cot.wait()
            lax.fori_loop(0, cot.shape[0] // 64, mask, 0)
        if u in LATE_ZL:
            copy_y0(u, par).wait_recv()
            copy_y2(u, par).start()
        else:
            copy_zl(u, par).wait_recv()
            copy_y1(u, par).start()

    def do_y2(u, par):
        if u in LATE_ZL:
            copy_y2(u, par).wait_recv()
            copy_zl(u, par).start()
        else:
            copy_y0(u, par).wait_recv()
            copy_y1(u, par).wait_recv()
            copy_y2(u, par).start()

    def do_core(u, par):
        (copy_zl if u in LATE_ZL else copy_y2)(u, par).wait_recv()
        copy_core(u, par).start()

    def do_fisher(u, par):
        copy_core(u, par).wait_recv()
        slot = u % SLOTS
        total = None
        for seq in range(seq_count):
            near, far = seq // 2, seq % 2
            order = (0, 1) if far == 0 else (1, 0)
            left = jnp.concatenate(
                [xt[near, far, a, c, u] for a in order for c in range(2)], axis=1)
            grad = jnp.dot(left, cot[seq * seq_len:(seq + 1) * seq_len, :], preferred_element_type=F32)
            total = grad * grad if total is None else total + grad * grad
        f32_f[slot] = total
        most = total[:, :LANES]
        for g in range(1, groups):
            most = jnp.maximum(most, total[:, g * LANES:(g + 1) * LANES])
        top = most[:TILE]
        for r in range(1, ROWS // TILE):
            top = jnp.maximum(top, most[r * TILE:(r + 1) * TILE])
        exponent = jnp.ceil(jnp.log2(jnp.maximum(top, 1e-30)) + 0.01).astype(I32).astype(I16)
        count = ROWS // 2 // TILE
        x1s[u, count * groups] = exponent
        inverse = wide(1.0 / scale_of(exponent), groups)
        base = (1 - bit[par]) * count

        def step(r, carry):
            code = code_d(f32_f[slot, rows(base + r, TILE)], inverse)
            for g in range(groups):
                x1s[u, r * groups + g] = code[:, g * LANES:(g + 1) * LANES]
            return carry

        lax.fori_loop(0, count, step, 0)
        copy_x1(u, par).start()

    def tiles(ref, u, at):
        return jnp.concatenate([ref[u, at + g] for g in range(groups)], axis=1)

    def do_x2(u, par):
        copy_x1(u, par).wait_recv()
        if u == 0:
            load_w.wait()
            for sort in range(2):
                weights(sort).wait_recv()
        slot = u % SLOTS
        count = ROWS // 2 // TILE
        half = count // 2
        e_own, e_rx = x1s[u, count * groups].astype(I32), x1r[u, count * groups].astype(I32)
        exponent = (jnp.maximum(e_own, e_rx) + 1).astype(I16)
        x2s[u, 2 * half * groups] = exponent
        inverse = wide(1.0 / scale_of(exponent), groups)
        scale = wide(scale_of(e_rx), groups)
        kept = bit[par] * count

        def both(r):
            f_own = f32_f[slot, rows(kept + r, TILE)]
            f_rx = read_d(tiles(x1r, u, r * groups), scale)
            own = w_own[u // 2, par, rows(kept + r, TILE)].astype(F32)
            other = w_rx[u // 2, par, rows(r, TILE)].astype(F32)
            return f_own + f_rx, f_own * own + f_rx * other

        def send(r, carry):
            denom, numer = both((1 - bit[1 - par]) * half + r)
            d, m = code_d(denom, inverse), code_r(numer, denom)
            for g in range(groups):
                x2s[u, r * groups + g] = d[:, g * LANES:(g + 1) * LANES]
                x2s[u, (half + r) * groups + g] = m[:, g * LANES:(g + 1) * LANES]
            return carry

        lax.fori_loop(0, half, send, 0)
        copy_x2(u, par).start()

        def keep(r, carry):
            denom, numer = both(bit[1 - par] * half + r)
            sums[slot, 0, rows(r, TILE)] = denom
            sums[slot, 1, rows(r, TILE)] = numer
            return carry

        lax.fori_loop(0, half, keep, 0)

    def put(ref, at, code):
        for g in range(groups):
            ref[at + g] = code[:, g * LANES:(g + 1) * LANES]

    def do_z(u, par):
        copy_x2(u, par).wait_recv()
        slot = u % SLOTS
        half = ROWS // 4 // TILE
        e_own, e_rx = x2s[u, 2 * half * groups].astype(I32), x2r[u, 2 * half * groups].astype(I32)
        exponent = (jnp.maximum(e_own, e_rx) + 1).astype(I16)
        inverse = wide(1.0 / scale_of(exponent), groups)
        scale = wide(scale_of(e_rx), groups)

        def four(at):
            d_rx = read_d(tiles(x2r, u, at * groups), scale)
            m_rx = read_r(tiles(x2r, u, (half + at) * groups))
            return sums[slot, 0, rows(at, TILE)] + d_rx, sums[slot, 1, rows(at, TILE)] + d_rx * m_rx

        if u in TREE_Z:
            for n in range(2):
                denom, numer = four((1 - z_bit[par]) * 2 + n)
                put(zas.at[u], n * groups, code_d(denom, inverse))
                put(zas.at[u], (2 + n) * groups, code_r(numer, denom))
            zas[u, 4 * groups] = exponent
            copy_za(u, par).start()
            for n in range(2):
                denom, numer = four(z_bit[par] * 2 + n)
                sums2[slot, 0, n * TILE:(n + 1) * TILE] = denom
                sums2[slot, 1, n * TILE:(n + 1) * TILE] = numer
            return
        for j in (2, 1, 3, 0):
            denom, numer = four(group((zh + j) % 4, par))
            if j == 0:
                mine[slot, 0] = denom
                mine[slot, 1] = numer
                continue
            put(zs.at[u, j - 1], 0, code_d(denom, inverse))
            put(zs.at[u, j - 1], groups, code_r(numer, denom))
            zs[u, j - 1, 2 * groups] = exponent
            copy_z(u, j).start()

    def do_zz(u, par):
        if u not in TREE_Z:
            return
        copy_za(u, par).wait_recv()
        slot = u % SLOTS
        e_own, e_rx = zas[u, 4 * groups].astype(I32), zar[u, 4 * groups].astype(I32)
        exponent = (jnp.maximum(e_own, e_rx) + 1).astype(I16)
        inverse = wide(1.0 / scale_of(exponent), groups)
        scale = wide(scale_of(e_rx), groups)

        def eight(at):
            d_rx = read_d(tiles(zar, u, at * groups), scale)
            m_rx = read_r(tiles(zar, u, (2 + at) * groups))
            return sums2[slot, 0, rows(at, TILE)] + d_rx, sums2[slot, 1, rows(at, TILE)] + d_rx * m_rx

        denom, numer = eight(1 - z_bit[1 - par])
        put(zs.at[u, 0], 0, code_d(denom, inverse))
        put(zs.at[u, 0], groups, code_r(numer, denom))
        zs[u, 0, 2 * groups] = exponent
        copy_zb(u, par).start()
        denom, numer = eight(z_bit[1 - par])
        mine[slot, 0] = denom
        mine[slot, 1] = numer

    def do_merge(u, par):
        slot = u % SLOTS
        denom, numer = mine[slot, 0], mine[slot, 1]
        for j in (1,) if u in TREE_Z else (1, 2, 3):
            (copy_zb(u, par) if u in TREE_Z else copy_z(u, j)).wait_recv()
            scale = wide(scale_of(zr[u, j - 1, 2 * groups].astype(I32)), groups)
            d_rx = read_d(jnp.concatenate([zr[u, j - 1, g] for g in range(groups)], axis=1), scale)
            m_rx = read_r(jnp.concatenate([zr[u, j - 1, groups + g] for g in range(groups)], axis=1))
            denom = denom + d_rx
            numer = numer + d_rx * m_rx
        region(u, par, 16)[...] = (numer / (denom + 1e-6)).astype(BF16)
        if u in TREE_B:
            copy_b1(u, par).start()
        else:
            for j in (2, 1, 3):
                copy_az(u, par, j).start()

    def do_b2(u, par):
        if u in TREE_B:
            copy_b1(u, par).wait_recv()
            copy_b2(u, par).start()

    def do_a1(u, par):
        if u in TREE_B:
            copy_b2(u, par).wait_recv()
        else:
            for j in (1, 2, 3):
                copy_az(u, par, j).wait_recv()
        if u in DIRECT_X:
            for copy in copies_ad(u, par):
                copy.start()
        else:
            copy_a1(u, par).start()

    def do_a2(u, par):
        if u not in DIRECT_X:
            copy_a1(u, par).wait_recv()
            copy_a2(u, par).start()

    def do_out(u, par):
        if u in DIRECT_X:
            for copy in copies_ad(u, par):
                copy.wait_recv()
        else:
            copy_a2(u, par).wait_recv()

    load_acts.wait()
    for u in range(TURNED):
        turn(u)
    pl.semaphore_wait(barrier, len(others))
    for par in range(2):
        weights(par).start()

    stages = (do_turn, do_y1, do_y2, do_core, do_fisher, do_x2, do_z, do_zz, do_merge,
              do_b2, do_a1, do_a2, do_out)
    for step in ORDER:
        stages[step // UNITS](step % UNITS, step % UNITS % 2)

    for par in range(2):
        weights(par).wait_send()

    for u in range(UNITS):
        par = u % 2
        sent = [copy_zl(u, par), copy_y0(u, par), copy_y2(u, par), copy_core(u, par),
                copy_x1(u, par), copy_x2(u, par)]
        if u not in LATE_ZL:
            sent.append(copy_y1(u, par))
        sent += [copy_za(u, par), copy_zb(u, par)] if u in TREE_Z else [copy_z(u, j) for j in (1, 2, 3)]
        sent += [copy_b1(u, par), copy_b2(u, par)] if u in TREE_B else [copy_az(u, par, j) for j in (1, 2, 3)]
        sent += copies_ad(u, par) if u in DIRECT_X else [copy_a1(u, par), copy_a2(u, par)]
        for copy in sent:
            copy.wait_send()


def body(acts, cotangent, seq_lengths, up_weight):
    tokens, cols = cotangent.shape[1:]
    width = acts.shape[2]
    groups = cols // LANES
    any_space = pl.BlockSpec(memory_space=pl.ANY)
    half, quarter = ROWS // 2 // TILE, ROWS // 4 // TILE
    merged = pl.pallas_call(
        kernel,
        out_shape=pltpu.VMEM((UNITS, ROWS, cols), BF16),
        in_specs=[pl.BlockSpec(memory_space=pltpu.SMEM), any_space, any_space, any_space],
        out_specs=pl.BlockSpec(memory_space=pltpu.VMEM),
        scratch_shapes=[
            pltpu.VMEM((acts.shape[1], width), BF16),
            pltpu.VMEM((2, 2, 2, 2, UNITS, ROWS, LANES), BF16),
            pltpu.VMEM((tokens, cols), BF16),
            pltpu.VMEM((UNITS // 2, 2, ROWS, cols), BF16),
            pltpu.VMEM((UNITS // 2, 2, ROWS // 2, cols), BF16),
            pltpu.VMEM((SLOTS, ROWS, cols), F32),
            pltpu.VMEM((SLOTS, 2, ROWS // 4, cols), F32),
            pltpu.VMEM((SLOTS, 2, 2 * TILE, cols), F32),
            pltpu.VMEM((SLOTS, 2, TILE, cols), F32),
            pltpu.VMEM((UNITS, half * groups + 1, TILE, LANES), I16),
            pltpu.VMEM((UNITS, half * groups + 1, TILE, LANES), I16),
            pltpu.VMEM((UNITS, 2 * quarter * groups + 1, TILE, LANES), I16),
            pltpu.VMEM((UNITS, 2 * quarter * groups + 1, TILE, LANES), I16),
            pltpu.VMEM((UNITS, 4 * groups + 1, TILE, LANES), I16),
            pltpu.VMEM((UNITS, 4 * groups + 1, TILE, LANES), I16),
            pltpu.VMEM((UNITS, 3, 2 * groups + 1, TILE, LANES), I16),
            pltpu.VMEM((UNITS, 3, 2 * groups + 1, TILE, LANES), I16),
            pltpu.SemaphoreType.DMA((3,)),
            pltpu.SemaphoreType.DMA((2,)),
            pltpu.SemaphoreType.DMA((2,)),
            pltpu.SemaphoreType.DMA((12, UNITS)),
            pltpu.SemaphoreType.DMA((12, UNITS)),
            pltpu.SemaphoreType.DMA((UNITS, 3)),
            pltpu.SemaphoreType.DMA((UNITS, 3)),
            pltpu.SemaphoreType.DMA((UNITS, 3)),
            pltpu.SemaphoreType.DMA((UNITS, 3)),
            pltpu.SemaphoreType.DMA((UNITS, 3)),
            pltpu.SemaphoreType.DMA((UNITS, 3)),
        ],
        compiler_params=pltpu.CompilerParams(
            collective_id=0, has_side_effects=True, vmem_limit_bytes=54 * 2**20),
    )(seq_lengths, acts[0], cotangent[0], up_weight[0].reshape(UNITS // 2, 2, ROWS, cols))
    return merged.reshape(width, cols)


def solution(mesh):
    in_specs = (
        P("ckpt", "tensor", None),
        P("ckpt", None, "tensor"),
        P(),
        P("ckpt", None, "tensor"),
    )
    out_specs = P(None, "tensor")
    return jax.shard_map(body, mesh=mesh, in_specs=in_specs, out_specs=out_specs, check_vma=False)
```
